128 devices in a mesh: seq: 16 (over y, z_lo, core), grp: 8 (over x, z_hi).
Axes of the slice: x: 4, y: 4, z: 4 (z_hi: 2, z_lo: 2; z = z_hi * 2 + z_lo), core: 2. Of those that a mesh axis runs over, the one named last changes fastest.
Arguments:
- tokens: bfloat16 [8, 4096, 768], P('grp', 'seq'), may hold values from -6 to 6
- sequence: int32 [8, 4096], P('grp'), may hold values from 0 to 4, as said below
- positions: int32 [8, 4096], P('grp'), may hold values from 0 to 2047, as said below
- first_gain: bfloat16 [768], replicated, may hold values from 0.5 to 1.5
- first_shift: bfloat16 [768], replicated, may hold values from -1.75 to 1.75
- input_weight: bfloat16 [768, 2304], replicated, may hold values from -0.21875 to 0.21875
- input_bias: bfloat16 [2304], replicated, may hold values from -1.75 to 1.75
- output_weight: bfloat16 [768, 768], replicated, may hold values from -3.5 to 3.5
- output_bias: bfloat16 [768], replicated, may hold values from -1.75 to 1.75
- second_gain: bfloat16 [768], replicated, may hold values from 0.5 to 1.5
- second_shift: bfloat16 [768], replicated, may hold values from -1.75 to 1.75
- up_weight: bfloat16 [768, 3072], replicated, may hold values from -0.21875 to 0.21875
- up_bias: bfloat16 [3072], replicated, may hold values from -1.75 to 1.75
- down_weight: bfloat16 [3072, 768], replicated, may hold values from -0.109375 to 0.109375
- down_bias: bfloat16 [768], replicated, may hold values from -1.75 to 1.75
- cotangent: bfloat16 [8, 4096, 768], P('grp', 'seq'), may hold values from -6 to 6
Outputs:
- result: bfloat16 [8, 4096, 768], P('grp', 'seq')
- grad_tokens: float32 [8, 4096, 768], P('grp', 'seq')
- grad_first_gain: float32 [768], replicated
- grad_first_shift: float32 [768], replicated
- grad_input_weight: float32 [768, 2304], replicated
- grad_input_bias: float32 [2304], replicated
- grad_output_weight: float32 [768, 768], replicated
- grad_output_bias: float32 [768], replicated
- grad_second_gain: float32 [768], replicated
- grad_second_shift: float32 [768], replicated
- grad_up_weight: float32 [768, 3072], replicated
- grad_up_bias: float32 [3072], replicated
- grad_down_weight: float32 [3072, 768], replicated
- grad_down_bias: float32 [768], replicated
The draws below stay inside these ranges and needn't reach their ends.
Inputs may be any that keep to these rules, and one draw needn't show every extreme that they name: In each group id 0 marks one sequence of 2048 tokens and ids 1 upward sequences of 512 tokens; taken block by block in some order of the seq devices, the group's tokens are the sequences laid end to end in order of id; the first and the last device along seq hold tokens of sequence 0. Each sequence's tokens carry the positions 0 up to its length minus 1 in order.
All inputs are finite; a program needn't handle non-finite values.
Results may differ from the reference program's by a relative error of at most 0.0095.
Values may be sent and summed in bfloat16 or wider, within the bound.
No kernel may reach another device: no remote copies, remote signals or barrier semaphores. Data moves between devices by JAX's collectives and lax.ppermute only.
A program may use at most 320 MiB of HBM per device.

```python
import math
import jax
import jax.numpy as jnp
from jax import lax

H = 12
DH = 64
D = 768
FF = 3072
ROT = 16
TOK_DEV = 256
SHORT = 512
GROUP_TOK = 4096
LONG = 2048
GROUPS = 8


def block_layout(key):
    blocks = GROUP_TOK // TOK_DEV
    group_keys = jax.random.split(key, GROUPS)
    ranks = jax.vmap(lambda one_key: jax.random.permutation(one_key, blocks))(group_keys).astype(jnp.int32)
    ranks = ranks.at[:, 0].set(-1).at[:, 1].set(blocks)
    order = jnp.argsort(ranks, axis=1, stable=True).astype(jnp.int32)
    logical = (order[:, :, None] * TOK_DEV + jnp.arange(TOK_DEV, dtype=jnp.int32)[None, None, :]).reshape(GROUPS, GROUP_TOK)
    later = logical - LONG
    ident = jnp.where(logical < LONG, 0, 1 + later // SHORT)
    places = jnp.where(logical < LONG, logical, later % SHORT)
    return (ident.astype(jnp.int32), places.astype(jnp.int32))


def draw_sequence(key, part):
    return block_layout(key)[0]


def draw_positions(key, part):
    return block_layout(key)[1]


def levels(own_key, shape, shards, smallest, largest):
    level = 1.0
    for dim, shards_of in shards:
        steps = jax.random.uniform(jax.random.fold_in(jax.random.fold_in(own_key, 6), dim), (shards_of,), jnp.float32, smallest / len(shards), largest / len(shards))
        level = level * jnp.repeat(jnp.exp(steps), shape[dim] // shards_of).reshape((-1,) + (1,) * (len(shape) - 1 - dim))
    return level


def scatter_about(own_key, extent, scale, reach, cuts=(), kind=jnp.bfloat16):
    array = jax.random.normal(own_key, extent, jnp.float32) * scale
    if len(cuts) > 0:
        array = levels(own_key, extent, cuts, -0.22, 0.18) * array
    return jnp.clip(array, min=-reach, max=reach).astype(kind)


def setup_inputs(seed: int = 0) -> dict:
    streams_of = jax.random.split(jax.random.key(seed), 17)
    tokens = scatter_about(streams_of[0], (GROUPS, GROUP_TOK, D), 1.0, 6.0, ((0, 8), (1, 16)))
    sequence = draw_sequence(jax.random.fold_in(streams_of[16], 71), 0)
    positions = draw_positions(jax.random.fold_in(streams_of[16], 71), 0)
    first_gain = jnp.clip(1.0 + 0.1 * jax.random.normal(streams_of[3], (D,), jnp.float32), 0.5, 1.5).astype(jnp.bfloat16)
    first_shift = scatter_about(streams_of[4], (D,), 0.3, 1.75)
    input_weight = scatter_about(streams_of[5], (D, 3 * D), D ** -0.5, 0.21875)
    input_bias = scatter_about(streams_of[6], (3 * D,), 0.3, 1.75)
    output_weight = scatter_about(streams_of[7], (D, D), (max(D // 256, 1)) ** -0.5, 3.5)
    output_bias = scatter_about(streams_of[8], (D,), 0.3, 1.75)
    second_gain = jnp.clip(1.0 + 0.1 * jax.random.normal(streams_of[9], (D,), jnp.float32), 0.5, 1.5).astype(jnp.bfloat16)
    second_shift = scatter_about(streams_of[10], (D,), 0.3, 1.75)
    up_weight = scatter_about(streams_of[11], (D, FF), D ** -0.5, 0.21875)
    up_bias = scatter_about(streams_of[12], (FF,), 0.3, 1.75)
    down_weight = scatter_about(streams_of[13], (FF, D), FF ** -0.5, 0.109375)
    down_bias = scatter_about(streams_of[14], (D,), 0.3, 1.75)
    cotangent = scatter_about(streams_of[15], (GROUPS, GROUP_TOK, D), 1.0, 6.0, ((0, 8), (1, 16)))
    return dict(tokens=tokens, sequence=sequence, positions=positions, first_gain=first_gain, first_shift=first_shift, input_weight=input_weight, input_bias=input_bias, output_weight=output_weight, output_bias=output_bias, second_gain=second_gain, second_shift=second_shift, up_weight=up_weight, up_bias=up_bias, down_weight=down_weight, down_bias=down_bias, cotangent=cotangent)


@jax.custom_vjp
def low(v):
    return lax.optimization_barrier(v.astype(jnp.bfloat16)).astype(jnp.float32)

@jax.custom_vjp
def low_back(v):
    return v

def low_keep(v):
    return (low(v), None)

def low_pass(kept, grad):
    return (grad,)

def back_keep(v):
    return (v, None)

def back_low(kept, grad):
    return (low(grad),)
low.defvjp(low_keep, low_pass)
low_back.defvjp(back_keep, back_low)
EPS = 1e-05
HIGHEST = lax.Precision.HIGHEST

def layer_norm(values, gain, shift):
    centre = values - lax.optimization_barrier(jnp.mean(values, axis=-1, keepdims=True))
    spread = lax.optimization_barrier(jnp.mean(centre * centre, axis=-1, keepdims=True))
    return centre * lax.rsqrt(spread + EPS) * gain + shift

def rotary_tables(places, width):
    half = width // 2
    freq = 1.0 / 10000.0 ** (jnp.arange(half, dtype=jnp.float32) * 2.0 / width)
    angle = places.astype(jnp.float32)[:, None] * freq[None, :]
    return (jnp.cos(angle)[:, None, :], jnp.sin(angle)[:, None, :])

def rotate(values, cosine, sine, width):
    half = width // 2
    first = values[..., :half]
    second = values[..., half:width]
    rest = values[..., width:]
    return jnp.concatenate([first * cosine - second * sine, second * cosine + first * sine, rest], axis=-1)

def masked_probs(scores, visible):
    scores = jnp.where(visible, scores, -1e+30)
    top = lax.optimization_barrier(jnp.max(scores, axis=-1, keepdims=True))
    raised = jnp.exp(scores - top)
    return raised / lax.optimization_barrier(jnp.sum(raised, axis=-1, keepdims=True))

def product(left, right):
    return jnp.dot(left, right, precision=HIGHEST)

def group_forward(weights, inputs, sequence, places):
    first_gain, first_shift, input_weight, input_bias, output_weight, output_bias, second_gain, second_shift, up_weight, up_bias, down_weight, down_bias = weights
    count = inputs.shape[0]
    width = inputs.shape[1]
    score_scale = 1.0 / math.sqrt(DH)
    normed_first = low(layer_norm(inputs, first_gain, first_shift))
    mixed = low_back(product(normed_first, input_weight) + input_bias)
    cosine, sine = rotary_tables(places, ROT)
    queries = low(rotate(mixed[:, :width].reshape(count, H, DH), cosine, sine, ROT))
    keys = low(rotate(mixed[:, width:2 * width].reshape(count, H, DH), cosine, sine, ROT))
    values = low(mixed[:, 2 * width:].reshape(count, H, DH))
    visible = (sequence[:, None] == sequence[None, :]) & (places[None, :] <= places[:, None])

    def attend(operands):
        query_one, key_one, value_one = operands
        scores = low_back(jnp.einsum('qd,kd->qk', query_one, key_one, precision=HIGHEST) * score_scale)
        weights_low = low(masked_probs(scores, visible))
        return jnp.einsum('qk,kd->qd', weights_low, value_one, precision=HIGHEST)
    attended = lax.map(jax.checkpoint(attend), (queries.transpose(1, 0, 2), keys.transpose(1, 0, 2), values.transpose(1, 0, 2)))
    attended = low(low_back(attended.transpose(1, 0, 2).reshape(count, width)))
    attn_out = product(attended, output_weight) + output_bias
    normed_second = low(layer_norm(inputs, second_gain, second_shift))
    hidden_pre = low_back(product(normed_second, up_weight) + up_bias)
    activated = low(jax.nn.gelu(hidden_pre, approximate=False))
    feed_out = product(activated, down_weight) + down_bias
    return inputs + attn_out + feed_out

def reference(tokens, sequence, positions, first_gain, first_shift, input_weight, input_bias, output_weight, output_bias, second_gain, second_shift, up_weight, up_bias, down_weight, down_bias, cotangent):
    weights = (first_gain.astype(jnp.float32), first_shift.astype(jnp.float32), input_weight.astype(jnp.float32), input_bias.astype(jnp.float32), output_weight.astype(jnp.float32), output_bias.astype(jnp.float32), second_gain.astype(jnp.float32), second_shift.astype(jnp.float32), up_weight.astype(jnp.float32), up_bias.astype(jnp.float32), down_weight.astype(jnp.float32), down_bias.astype(jnp.float32))
    inputs = tokens.astype(jnp.float32)

    def forward(inputs_all, weights_all):

        def one_group(operands):
            group_inputs, group_sequence, group_places = operands
            return group_forward(weights_all, group_inputs, group_sequence, group_places)
        return lax.map(jax.checkpoint(one_group), (inputs_all, sequence, positions))
    outputs, pullback = jax.vjp(forward, inputs, weights)
    grad_inputs, grads = pullback(cotangent.astype(jnp.float32))
    return (outputs.astype(jnp.bfloat16), grad_inputs, grads[0], grads[1], grads[2], grads[3], grads[4], grads[5], grads[6], grads[7], grads[8], grads[9], grads[10], grads[11])
```

```python
import math

import jax
import jax.numpy as jnp
import numpy as np
from jax import lax
from jax.experimental import pallas as pl
from jax.experimental.pallas import tpu as pltpu
from jax.sharding import PartitionSpec as P

H = 12
DH = 64
D = 768
FF = 3072
ROT = 16
TOK = 256
SEQ_DEV = 16
LONG_BLOCKS = 8
EPS = 1e-05
F32 = jnp.float32
BF16 = jnp.bfloat16
TILE = 512


def place(index):
    seq, grp = index // 8, index % 8
    return {
        "x": grp // 2,
        "y": seq // 4,
        "z": (grp % 2) * 2 + (seq // 2) % 2,
        "c": seq % 2,
    }


def index_of(at):
    seq = at["y"] * 4 + (at["z"] % 2) * 2 + at["c"]
    grp = at["x"] * 2 + at["z"] // 2
    return seq * 8 + grp


def swap(value, partner):
    pairs = [(i, index_of(partner(place(i)))) for i in range(128)]
    return lax.ppermute(value, ("seq", "grp"), pairs)


def here():
    seq, grp = lax.axis_index("seq"), lax.axis_index("grp")
    return {
        "x": grp // 2,
        "y": seq // 4,
        "z": (grp % 2) * 2 + (seq // 2) % 2,
        "c": seq % 2,
    }


def other_core(at):
    return {**at, "c": 1 - at["c"]}


def ring_partner(axis, step):
    def partner(at):
        i = at[axis]
        return {**at, axis: i ^ 1 if step == at["c"] else 3 - i}

    return partner


def ring_bits(i, core):
    inner = ((i == 1) | (i == 2)).astype(jnp.int32)
    upper = (i >= 2).astype(jnp.int32)
    return jnp.where(core == 0, inner, upper), jnp.where(core == 0, upper, inner)


def half(value, which):
    rows = value.shape[0] // 2
    return lax.dynamic_slice_in_dim(value, which * rows, rows, 0)


def ring_scatter(value, axis, at):
    for step, bit in enumerate(ring_bits(at[axis], at["c"])):
        got = swap(half(value, 1 - bit), ring_partner(axis, step))
        value = (half(value, bit).astype(F32) + got.astype(F32)).astype(BF16)
    return value


def ring_gather(value, axis, at, ordered):
    bits = ring_bits(at[axis], at["c"])
    for step in (1, 0):
        got = swap(value, ring_partner(axis, step))
        if ordered:
            first = jnp.where(bits[step] == 0, value, got)
            second = jnp.where(bits[step] == 0, got, value)
            value = jnp.concatenate([first, second], 0)
        else:
            value = jnp.concatenate([value, got], 0)
    return value


def contract(left, right, dims):
    return lax.dot_general(left, right, (dims, ((), ())), preferred_element_type=F32)


def rotate_rows(rows, cosine, sine):
    first, second = rows[0:8], rows[8:16]
    return jnp.concatenate(
        [first * cosine - second * sine, second * cosine + first * sine, rows[16:]], 0
    )


def head_kernel(
    logical, place_block, live,
    rows_ref, table_ref, w_ref, wo_ref, bias_ref, norm_ref, extra_ref,
    send_ref, grad_ref,
    t_ref, q_ref, k_ref, v_ref, g_ref, s_ref, p_ref, dk_ref, dv_ref, o_ref, gw_ref, go_ref, gb_ref, gc_ref,
):
    def project(b, _):
        at = pl.multiple_of(b * TOK, TOK)
        to = pl.multiple_of(logical[b] * TOK, TOK)
        pos = pl.multiple_of(place_block[b] * TOK, TOK)
        cosine = table_ref[0:8, pl.ds(pos, TOK)]
        sine = table_ref[8:16, pl.ds(pos, TOK)]
        mixed = contract(w_ref[...], rows_ref[pl.ds(at, TOK), 0:D], ((1,), (1,)))
        mixed = mixed + bias_ref[:, 0:1]
        query = rotate_rows(mixed[0:64], cosine, sine) * 0.125
        key = rotate_rows(mixed[64:128], cosine, sine)
        value = mixed[128:192]
        grad = contract(wo_ref[...], rows_ref[pl.ds(at, TOK), D:], ((1,), (1,)))
        for n, (part, ref) in enumerate(
            ((query, q_ref), (key, k_ref), (value, v_ref), (grad, g_ref))
        ):
            t_ref[n * 64 : n * 64 + 64, pl.ds(to, TOK)] = part.astype(BF16)
            ref[pl.ds(to, TOK), :] = part.T.astype(BF16)
        return 0

    lax.fori_loop(0, SEQ_DEV, project, 0)
    dk_ref[...] = jnp.zeros_like(dk_ref)
    dv_ref[...] = jnp.zeros_like(dv_ref)

    def attend(task, _):
        base = pl.multiple_of(task * TILE, TILE)
        full = jnp.where(task < 4, task, 0)
        q_t = t_ref[0:64, pl.ds(base, TILE)]
        g_t = t_ref[192:256, pl.ds(base, TILE)]

        def score(keys, slot, top, masked):
            scores = contract(k_ref[pl.ds(keys, TILE), :], q_t, ((1,), (0,)))
            if masked:
                key_at = lax.broadcasted_iota(jnp.int32, (TILE, TILE), 0)
                query_at = lax.broadcasted_iota(jnp.int32, (TILE, TILE), 1)
                scores = jnp.where(key_at <= query_at, scores, -1e30)
            s_ref[pl.ds(slot, TILE), :] = scores
            return jnp.maximum(top, jnp.max(scores, axis=0, keepdims=True))

        last = pl.multiple_of(full * TILE, TILE)
        top = score(base, last, jnp.full((1, TILE), -1e30, F32), True)

        def score_step(j, top):
            at = pl.multiple_of(j * TILE, TILE)
            return score(at, at, top, False)

        top = lax.fori_loop(0, full, score_step, top)

        def weigh(keys, slot, carry):
            total, dot_total, out = carry
            raised = jnp.exp(s_ref[pl.ds(slot, TILE), :] - top)
            s_ref[pl.ds(slot, TILE), :] = raised
            grads = contract(v_ref[pl.ds(keys, TILE), :], g_t, ((1,), (0,)))
            p_ref[pl.ds(slot, TILE), :] = grads
            total = total + jnp.sum(raised, axis=0, keepdims=True)
            dot_total = dot_total + jnp.sum(raised * grads, axis=0, keepdims=True)
            out = out + contract(
                t_ref[128:192, pl.ds(keys, TILE)], raised.astype(BF16), ((1,), (0,))
            )
            return total, dot_total, out

        carry = (jnp.zeros((1, TILE), F32), jnp.zeros((1, TILE), F32), jnp.zeros((64, TILE), F32))
        carry = weigh(base, last, carry)

        def weigh_step(j, carry):
            at = pl.multiple_of(j * TILE, TILE)
            return weigh(at, at, carry)

        total, dot_total, out = lax.fori_loop(0, full, weigh_step, carry)
        scale = 1.0 / total
        row_total = dot_total * scale
        o_ref[0:64, pl.ds(base, TILE)] = (out * scale).astype(BF16)

        def back(keys, slot, grad_q):
            probs = s_ref[pl.ds(slot, TILE), :] * scale
            grads = probs * (p_ref[pl.ds(slot, TILE), :] - row_total)
            grads = grads.astype(BF16)
            dv_ref[pl.ds(keys, TILE), :] += contract(
                probs.astype(BF16), g_ref[pl.ds(base, TILE), :], ((1,), (0,))
            )
            dk_ref[pl.ds(keys, TILE), :] += contract(
                grads, q_ref[pl.ds(base, TILE), :], ((1,), (0,))
            )
            return grad_q + contract(t_ref[64:128, pl.ds(keys, TILE)], grads, ((1,), (0,)))

        grad_q = back(base, last, jnp.zeros((64, TILE), F32))

        def back_step(j, grad_q):
            at = pl.multiple_of(j * TILE, TILE)
            return back(at, at, grad_q)

        grad_q = lax.fori_loop(0, full, back_step, grad_q) * 0.125
        cosine = table_ref[0:8, pl.ds(last, TILE)]
        sine = table_ref[8:16, pl.ds(last, TILE)]
        o_ref[64:128, pl.ds(base, TILE)] = rotate_rows(grad_q, cosine, -sine).astype(BF16)
        return 0

    lax.fori_loop(0, 8, attend, 0)

    def turn_back(task, _):
        base = pl.multiple_of(task * TILE, TILE)
        pos = pl.multiple_of(jnp.where(task < 4, task, 0) * TILE, TILE)
        cosine = table_ref[0:8, pl.ds(pos, TILE)]
        sine = table_ref[8:16, pl.ds(pos, TILE)]
        grad_k = dk_ref[pl.ds(base, TILE), :].T
        o_ref[128:192, pl.ds(base, TILE)] = rotate_rows(grad_k, cosine, -sine).astype(BF16)
        o_ref[192:256, pl.ds(base, TILE)] = dv_ref[pl.ds(base, TILE), :].T.astype(BF16)
        return 0

    lax.fori_loop(0, 8, turn_back, 0)
    gw_ref[...] = jnp.zeros_like(gw_ref)
    go_ref[...] = jnp.zeros_like(go_ref)
    gb_ref[...] = jnp.zeros_like(gb_ref)
    gc_ref[...] = jnp.zeros_like(gc_ref)

    def collect(b, _):
        at = pl.multiple_of(b * TOK, TOK)
        frm = pl.multiple_of(logical[b] * TOK, TOK)
        block = o_ref[:, pl.ds(frm, TOK)]
        send_ref[b] = block
        grads = block[64:256]
        gw_ref[...] += contract(grads, rows_ref[pl.ds(at, TOK), 0:D], ((1,), (0,)))
        go_ref[...] += contract(block[0:64], rows_ref[pl.ds(at, TOK), D:], ((1,), (0,)))
        gb_ref[...] += contract(jnp.ones((8, TOK), BF16), grads, ((1,), (1,)))
        gc_ref[...] += jnp.broadcast_to(
            jnp.sum(grads.astype(F32), axis=1, keepdims=True), (192, 128)
        )
        return 0

    lax.fori_loop(0, SEQ_DEV, collect, 0)
    grad_ref[0:192, :] = gw_ref[...].astype(BF16)
    grad_ref[192:256, :] = go_ref[...].astype(BF16)
    alive = live[0].astype(F32)
    weights = w_ref[...].astype(F32)
    sums = gc_ref[:, 0:1]
    shift_grad = jnp.sum(sums * weights, axis=0, keepdims=True) * alive
    gain_grad = jnp.sum(
        weights * (gw_ref[...] - sums * norm_ref[1:2, :]), axis=0, keepdims=True
    ) * alive / norm_ref[0:1, :]
    bias_row = jnp.concatenate([gb_ref[0:1, :], jnp.zeros((1, D - 192), F32)], 1) * alive
    grad_ref[256:272, :] = jnp.concatenate(
        [gain_grad, shift_grad, bias_row, jnp.zeros((5, D), F32), extra_ref[...]], 0
    ).astype(BF16)


def one_head(logical, place_block, live, rows, table, w_t, wo, bias, norm, extra):
    count = SEQ_DEV * TOK
    vmem = pl.BlockSpec(memory_space=pltpu.VMEM)
    return pl.pallas_call(
        head_kernel,
        out_shape=(
            jax.ShapeDtypeStruct((SEQ_DEV, 256, TOK), BF16),
            jax.ShapeDtypeStruct((272, D), BF16),
        ),
        grid_spec=pltpu.PrefetchScalarGridSpec(
            num_scalar_prefetch=3,
            grid=(),
            in_specs=[vmem] * 7,
            out_specs=(vmem, vmem),
            scratch_shapes=[
                pltpu.VMEM((256, count), BF16),
                pltpu.VMEM((count, DH), BF16),
                pltpu.VMEM((count, DH), BF16),
                pltpu.VMEM((count, DH), BF16),
                pltpu.VMEM((count, DH), BF16),
                pltpu.VMEM((4 * TILE, TILE), F32),
                pltpu.VMEM((4 * TILE, TILE), F32),
                pltpu.VMEM((count, DH), F32),
                pltpu.VMEM((count, DH), F32),
                pltpu.VMEM((256, count), BF16),
                pltpu.VMEM((192, D), F32),
                pltpu.VMEM((64, D), F32),
                pltpu.VMEM((8, 192), F32),
                pltpu.VMEM((192, 128), F32),
            ],
        ),
        compiler_params=pltpu.CompilerParams(vmem_limit_bytes=56 * 2**20),
        cost_estimate=pl.CostEstimate(
            flops=40 * 10**9, bytes_accessed=16 * 10**6, transcendentals=4 * 10**6
        ),
    )(logical, place_block, live, rows, table, w_t, wo, bias, norm, extra)


def rotary_table():
    freq = (1.0 / 10000.0 ** (np.arange(8, dtype=np.float64) * 2.0 / ROT)).astype(np.float32)
    angle = np.arange(2048, dtype=np.float32)[None, :] * freq[:, None]
    angle = angle.astype(np.float64)
    return np.concatenate([np.cos(angle), np.sin(angle)], 0).astype(np.float32)


def place_feed_kernel(own_chunk, mine_ref, theirs_ref, down_ref, up_ref):
    def put(block):
        down_ref[...] = block[:, 0:D].astype(F32)
        up_ref[...] = block[:, D:].astype(F32).T

    step = pl.program_id(0)

    @pl.when(step < 4)
    def _():
        put(mine_ref[...])

    @pl.when(step >= 4)
    def _():
        put(theirs_ref[...])


def place_feed(own_chunk, mine, theirs):
    rows = FF // 8

    def spot(step, where):
        own = step < 4
        core = jnp.where(own, where[2], 1 - where[2])
        chunk = jnp.where(own, where[0], where[1])
        return core * 4 + ((step % 4) ^ chunk)

    return pl.pallas_call(
        place_feed_kernel,
        out_shape=(
            jax.ShapeDtypeStruct((FF, D), F32),
            jax.ShapeDtypeStruct((D, FF), F32),
        ),
        grid_spec=pltpu.PrefetchScalarGridSpec(
            num_scalar_prefetch=1,
            grid=(8,),
            in_specs=[
                pl.BlockSpec((rows, 2 * D), lambda s, w: (jnp.minimum(s, 3), 0)),
                pl.BlockSpec((rows, 2 * D), lambda s, w: (jnp.maximum(s - 4, 0), 0)),
            ],
            out_specs=(
                pl.BlockSpec((rows, D), lambda s, w: (spot(s, w), 0)),
                pl.BlockSpec((D, rows), lambda s, w: (0, spot(s, w))),
            ),
        ),
        compiler_params=pltpu.CompilerParams(vmem_limit_bytes=40 * 2**20),
        cost_estimate=pl.CostEstimate(flops=0, bytes_accessed=28 * 10**6, transcendentals=0),
    )(own_chunk, mine, theirs)


def norm_parts(values):
    centre = values - jnp.mean(values, axis=-1, keepdims=True)
    spread = jnp.mean(centre * centre, axis=-1, keepdims=True)
    rate = lax.rsqrt(spread + EPS)
    return centre * rate, rate


def norm_back(normal, rate, grad, gain):
    scaled = grad * gain
    return rate * (
        scaled
        - jnp.mean(scaled, axis=-1, keepdims=True)
        - normal * jnp.mean(scaled * normal, axis=-1, keepdims=True)
    )


def gelu_and_slope(values):
    cdf = 0.5 * (1.0 + lax.erf(values * np.float32(math.sqrt(0.5))))
    pdf = jnp.exp(-0.5 * values * values) * np.float32(1.0 / math.sqrt(2.0 * math.pi))
    return values * cdf, cdf + values * pdf


def body(
    tokens,
    sequence,
    positions,
    first_gain,
    first_shift,
    input_weight,
    input_bias,
    output_weight,
    output_bias,
    second_gain,
    second_shift,
    up_weight,
    up_bias,
    down_weight,
    down_bias,
    cotangent,
):
    at = here()
    seq = lax.axis_index("seq")
    core = at["c"]
    inputs = tokens[0].astype(F32)
    grad_rows = cotangent[0]
    grad_float = grad_rows.astype(F32)
    gain_one, shift_one = first_gain.astype(F32), first_shift.astype(F32)
    gain_two, shift_two = second_gain.astype(F32), second_shift.astype(F32)
    normal, rate = norm_parts(inputs)
    normed_first = (normal * gain_one + shift_one).astype(BF16)
    normed_second = (normal * gain_two + shift_two).astype(BF16)

    with jax.named_scope("gather_rows"):
        rows_all = lax.all_gather(
            jnp.concatenate([normed_first, grad_rows], 1), "seq", axis=0, tiled=True
        )

    with jax.named_scope("feed"):
        own = jnp.concatenate([normed_second, grad_rows], 1)
        both = jnp.concatenate([own, swap(own, other_core)], 0)
        units = FF // 2
        up_half = lax.dynamic_slice_in_dim(up_weight, core * units, units, 1)
        down_half = lax.dynamic_slice_in_dim(down_weight, core * units, units, 0)
        bias_half = lax.dynamic_slice_in_dim(up_bias, core * units, units, 0).astype(F32)
        second_both, grad_both = both[:, :D], both[:, D:]
        hidden = contract(second_both, up_half, ((1,), (0,))) + bias_half
        active, slope = gelu_and_slope(hidden)
        active = active.astype(BF16)
        grad_hidden = (contract(grad_both, down_half, ((1,), (1,))) * slope).astype(BF16)
        grad_down = contract(active, grad_both, ((0,), (0,))).astype(BF16)
        grad_up = contract(grad_hidden, second_both, ((0,), (0,))).astype(BF16)
        feed_sum = jnp.concatenate([grad_down, grad_up], 1)
        up_bias_part = jnp.sum(grad_hidden.astype(F32), axis=0)
        feed_part = contract(active, down_half, ((1,), (0,)))
        back_part = contract(grad_hidden, up_half, ((1,), (1,)))
        parts = jnp.concatenate([feed_part, back_part], 1)
        got = swap(parts[TOK:].astype(BF16), other_core).astype(F32)
        parts = parts[:TOK] + got
        feed_out = parts[:, :D] + down_bias.astype(F32)
        grad_second = parts[:, D:]
        grad_second_inputs = norm_back(normal, rate, grad_second, gain_two)
        extra = jnp.concatenate(
            [
                jnp.sum(grad_float, axis=0)[None],
                jnp.sum(grad_second * normal, axis=0)[None],
                jnp.sum(grad_second, axis=0)[None],
                up_bias_part.reshape(2, D),
                jnp.zeros((3, D), F32),
            ],
            0,
        )

    with jax.named_scope("feed_scatter"):
        for axis in ("x", "y", "z"):
            feed_sum = ring_scatter(feed_sum, axis, at)

    with jax.named_scope("head"):
        starts = jnp.arange(SEQ_DEV) * TOK
        ids, places = sequence[0][starts], positions[0][starts] // TOK
        logical = jnp.where(ids == 0, places, LONG_BLOCKS + 2 * (ids - 1) + places)
        head = jnp.minimum(seq, H - 1)
        live = (seq < H).astype(jnp.int32)[None]
        cut = [
            lax.dynamic_slice_in_dim(input_weight, n * D + head * DH, DH, 1) for n in range(3)
        ]
        cut_bias = [
            lax.dynamic_slice_in_dim(input_bias, n * D + head * DH, DH, 0) for n in range(3)
        ]
        w_t = jnp.concatenate(cut, 1).T
        bias = jnp.broadcast_to(jnp.concatenate(cut_bias).astype(F32)[:, None], (192, 128))
        wo = lax.dynamic_slice_in_dim(output_weight, head * DH, DH, 0)
        norm = jnp.concatenate([gain_one[None], shift_one[None], jnp.zeros((6, D), F32)], 0)
        send, head_sum = one_head(
            logical.astype(jnp.int32),
            places.astype(jnp.int32),
            live,
            rows_all,
            jnp.asarray(rotary_table()),
            w_t,
            wo,
            bias,
            norm,
            extra,
        )

    with jax.named_scope("head_sum"):
        for partner in (
            ring_partner("x", 0),
            ring_partner("x", 1),
            lambda p: {**p, "z": p["z"] ^ 2},
        ):
            got = swap(head_sum, partner)
            head_sum = (head_sum.astype(F32) + got.astype(F32)).astype(BF16)
        sums = lax.all_gather(head_sum, "seq", axis=0)

    with jax.named_scope("heads_back"):
        got = lax.all_to_all(send, "seq", 0, 0, tiled=True)[:H]
        attended = got[:, 0:64].reshape(D, TOK)
        grad_mixed = got[:, 64:].reshape(H, 3, DH, TOK).transpose(1, 0, 2, 3).reshape(3 * D, TOK)
        attn_out = contract(attended, output_weight, ((0,), (0,))) + output_bias.astype(F32)
        result = (inputs + attn_out + feed_out).astype(BF16)[None]
        grad_first = contract(grad_mixed, input_weight, ((0,), (1,)))
        grad_first_inputs = norm_back(normal, rate, grad_first, gain_one)
        grad_tokens = (grad_float + grad_first_inputs + grad_second_inputs)[None]

    with jax.named_scope("feed_gather"):
        for axis, ordered in (("z", True), ("y", True), ("x", False)):
            feed_sum = ring_gather(feed_sum, axis, at, ordered)
        theirs = swap(feed_sum, other_core)
        chunks = []
        for which in (core, 1 - core):
            first, second = ring_bits(at["x"], which)
            chunks.append(first * 2 + second)
        where = jnp.stack([*chunks, core]).astype(jnp.int32)
        grad_down_weight, grad_up_weight = place_feed(where, feed_sum, theirs)

    with jax.named_scope("head_place"):
        heads = sums[:H].astype(F32)
        grad_input_weight = (
            heads[:, 0:192].reshape(H, 3, DH, D).transpose(3, 1, 0, 2).reshape(D, 3 * D)
        )
        grad_output_weight = heads[:, 192:256].reshape(D, D)
        rest = sums[:, 256:].astype(F32)
        grad_input_bias = (
            rest[:H, 2, :192].reshape(H, 3, DH).transpose(1, 0, 2).reshape(3 * D)
        )
        added = jnp.sum(rest, axis=0)
        up_rows = jnp.sum(rest[:, 11:13].reshape(SEQ_DEV // 2, 2, 2 * D), axis=0)
        grad_up_bias = up_rows.reshape(FF)
    return (
        result,
        grad_tokens,
        added[0],
        added[1],
        grad_input_weight,
        grad_input_bias,
        grad_output_weight,
        added[8],
        added[9],
        added[10],
        grad_up_weight,
        grad_up_bias,
        grad_down_weight,
        added[8],
    )


def solution(mesh):
    split = P("grp", "seq", None)
    in_specs = (split, P("grp", None), P("grp", None), *(P(),) * 12, split)
    out_specs = (split, split, *(P(),) * 12)
    return jax.shard_map(body, mesh=mesh, in_specs=in_specs, out_specs=out_specs, check_vma=False)
```

```python
import math

import jax
import jax.numpy as jnp
import numpy as np
from jax import lax
from jax.experimental import pallas as pl
from jax.experimental.pallas import tpu as pltpu
from jax.sharding import PartitionSpec as P

H = 12
DH = 64
D = 768
FF = 3072
ROT = 16
TOK = 256
SEQ_DEV = 16
LONG_BLOCKS = 8
EPS = 1e-05
F32 = jnp.float32
BF16 = jnp.bfloat16
TILE = 512
PROJECT = 4
COLLECT = 4
AHEAD = 8
FEED_CUT = 384
HEAD_ROWS = 272


AXES = ("y", "zl", "c", "x", "zh")
SIZES = (4, 2, 2, 4, 2)
SEQ = ("y", "zl", "c")


def place(index):
    at = {}
    for name, size in zip(reversed(AXES), reversed(SIZES)):
        index, at[name] = divmod(index, size)
    return at


def index_of(at):
    index = 0
    for name, size in zip(AXES, SIZES):
        index = index * size + at[name]
    return index


def swap(value, partner):
    pairs = [(i, index_of(partner(place(i)))) for i in range(math.prod(SIZES))]
    return lax.ppermute(value, AXES, pairs)


def here():
    return {name: lax.axis_index(name) for name in AXES}


def other(axis):
    return lambda at: {**at, axis: 1 - at[axis]}


def ring_next(i, core, step):
    near, far = i ^ 1, 3 - i
    if isinstance(core, int):
        return near if step == core else far
    return jnp.where(core == step, near, far)


def ring_partner(axis, step):
    return lambda at: {**at, axis: ring_next(at[axis], at["c"], step)}


def ring_bits(i, core):
    inner = ((i == 1) | (i == 2)).astype(jnp.int32)
    upper = (i >= 2).astype(jnp.int32)
    return jnp.where(core == 0, inner, upper), jnp.where(core == 0, upper, inner)


def ring_chunk(i, core):
    first, second = ring_bits(i, core)
    return first * 2 + second


def ring_slots(i, core):
    one, two = ring_next(i, core, 1), ring_next(i, core, 0)
    return [i, one, two, ring_next(two, core, 1)]


def added(*values):
    total = values[0].astype(F32)
    for value in values[1:]:
        total = total + value.astype(F32)
    return total.astype(BF16)


def half(value, which):
    rows = value.shape[1] // 2
    return lax.dynamic_slice_in_dim(value, which * rows, rows, 1)


def after(value, *earlier):
    return lax.optimization_barrier((value, *earlier))[0]


def norm_kernel(
    x_ref, grad_ref, gain1_ref, shift1_ref, gain2_ref, shift2_ref,
    rows_ref, own_ref, normal_ref, rate_ref,
):
    def row(ref):
        return ref[...].astype(F32).reshape(1, D)

    values = x_ref[...].astype(F32)
    centre = values - jnp.mean(values, axis=-1, keepdims=True)
    spread = jnp.mean(centre * centre, axis=-1, keepdims=True)
    rate = lax.rsqrt(spread + EPS)
    normal = centre * rate
    rows_ref[:, :D] = (normal * row(gain1_ref) + row(shift1_ref)).astype(BF16)
    own_ref[:, :D] = (normal * row(gain2_ref) + row(shift2_ref)).astype(BF16)
    rows_ref[:, D:] = grad_ref[...]
    own_ref[:, D:] = grad_ref[...]
    normal_ref[...] = normal
    rate_ref[...] = jnp.broadcast_to(rate, (TOK, 128))


def norms(x, grad_rows, gains):
    return pl.pallas_call(
        norm_kernel,
        out_shape=(
            jax.ShapeDtypeStruct((TOK, 2 * D), BF16),
            jax.ShapeDtypeStruct((TOK, 2 * D), BF16),
            jax.ShapeDtypeStruct((TOK, D), F32),
            jax.ShapeDtypeStruct((TOK, 128), F32),
        ),
        cost_estimate=pl.CostEstimate(
            flops=3 * 10**8, bytes_accessed=5 * 10**6, transcendentals=256
        ),
    )(x, grad_rows, *gains)


def contract(left, right, dims):
    return lax.dot_general(left, right, (dims, ((), ())), preferred_element_type=F32)


def rotate_rows(rows, cosine, sine):
    first, second = rows[0:8], rows[8:16]
    return jnp.concatenate(
        [first * cosine - second * sine, second * cosine + first * sine, rows[16:]], 0
    )


def head_kernel(
    ids, places, which,
    rows_hbm, table_ref, wo_ref, wq_ref, wk_ref, wv_ref, bq_ref, bk_ref, bv_ref, norm_ref, extra_ref,
    send_hbm, grad_ref,
    rows_ref, in_sem, out_sem, w_ref, bias_ref, t_ref, q_ref, k_ref, v_ref, g_ref, s_ref, p_ref, dk_ref, dv_ref, o_ref, gw_ref, go_ref, gb_ref, gc_ref,
):
    def place_block(b):
        return lax.div(places[b * TOK], TOK)

    def logical(b):
        ident = ids[b * TOK]
        return place_block(b) + jnp.where(ident == 0, 0, LONG_BLOCKS + 2 * (ident - 1))

    def fetch(b):
        at = pl.multiple_of(b * TOK, TOK)
        return pltpu.make_async_copy(
            rows_hbm.at[pl.ds(at, TOK)], rows_ref.at[pl.ds(at, TOK)], in_sem.at[b]
        )

    def post(b):
        frm = pl.multiple_of(logical(b) * TOK, TOK)
        return pltpu.make_async_copy(
            o_ref.at[:, pl.ds(frm, TOK)], send_hbm.at[b], out_sem.at[b]
        )

    for b in range(AHEAD):
        fetch(b).start()
    odd = which[0] % 2 == 1
    for n, (w, bias) in enumerate(((wq_ref, bq_ref), (wk_ref, bk_ref), (wv_ref, bv_ref))):
        block = jnp.where(odd, w[:, DH:].astype(F32), w[:, :DH].astype(F32))
        w_ref[n * DH : n * DH + DH, :] = block.T.astype(BF16)
        row = jnp.where(odd, bias[:, DH:], bias[:, :DH])
        bias_ref[n * DH : n * DH + DH, :] = jnp.broadcast_to(row, (128, DH)).T

    def project(step, _):
        for n in range(PROJECT):
            fetch(step * PROJECT + n).wait()

        for n in range(PROJECT):
            ahead = step * PROJECT + n + AHEAD

            @pl.when(ahead < SEQ_DEV)
            def _():
                fetch(ahead).start()

        at = pl.multiple_of(step * PROJECT * TOK, TOK)
        rows = rows_ref[pl.ds(at, PROJECT * TOK), :]
        mixed_all = contract(w_ref[...], rows[:, :D], ((1,), (1,))) + bias_ref[:, 0:1]
        grad_all = contract(wo_ref[...], rows[:, D:], ((1,), (1,)))
        for n in range(PROJECT):
            b = step * PROJECT + n
            to = pl.multiple_of(logical(b) * TOK, TOK)
            pos = pl.multiple_of(place_block(b) * TOK, TOK)
            cosine = table_ref[0:8, pl.ds(pos, TOK)]
            sine = table_ref[8:16, pl.ds(pos, TOK)]
            mixed = mixed_all[:, n * TOK : n * TOK + TOK]
            query = rotate_rows(mixed[0:64], cosine, sine) * 0.125
            key = rotate_rows(mixed[64:128], cosine, sine)
            parts = (query, key, mixed[128:192], grad_all[:, n * TOK : n * TOK + TOK])
            for m, (part, ref) in enumerate(zip(parts, (q_ref, k_ref, v_ref, g_ref))):
                part = part.astype(BF16)
                t_ref[m * 64 : m * 64 + 64, pl.ds(to, TOK)] = part
                ref[pl.ds(to, TOK), :] = part.T
        return 0

    lax.fori_loop(0, SEQ_DEV // PROJECT, project, 0)

    def attend(task):
        base = task * TILE
        full = task if task < 4 else 0
        last = full * TILE
        small = TILE // 2
        corner = (
            (base, last, 0, True),
            (base + small, last + small, small, True),
        )

        def keys_of(part):
            return pl.ds(part[0], small if part[3] else TILE)

        def slot_of(part):
            return pl.ds(part[1], small if part[3] else TILE)

        def lanes(part):
            return slice(part[2], TILE)

        def widen(part, value, fill):
            if part[2] == 0:
                return value
            return jnp.concatenate([jnp.full(value.shape, fill, F32), value], 1)

        q_t = t_ref[0:64, pl.ds(base, TILE)]
        g_t = t_ref[192:256, pl.ds(base, TILE)]

        def score(part, top):
            scores = contract(k_ref[keys_of(part), :], q_t[:, lanes(part)], ((1,), (0,)))
            if part[3]:
                key_at = lax.broadcasted_iota(jnp.int32, scores.shape, 0)
                query_at = lax.broadcasted_iota(jnp.int32, scores.shape, 1)
                scores = jnp.where(key_at <= query_at, scores, -1e30)
            s_ref[slot_of(part), lanes(part)] = scores
            return jnp.maximum(top, widen(part, jnp.max(scores, axis=0, keepdims=True), -1e30))

        def weigh(part, carry):
            total, dot_total, out = carry
            raised = jnp.exp(s_ref[slot_of(part), lanes(part)] - top[:, lanes(part)])
            s_ref[slot_of(part), lanes(part)] = raised
            grads = contract(v_ref[keys_of(part), :], g_t[:, lanes(part)], ((1,), (0,)))
            p_ref[slot_of(part), lanes(part)] = grads
            total = total + widen(part, jnp.sum(raised, axis=0, keepdims=True), 0.0)
            dot_total = dot_total + widen(
                part, jnp.sum(raised * grads, axis=0, keepdims=True), 0.0
            )
            out = out + widen(
                part,
                contract(t_ref[128:192, keys_of(part)], raised.astype(BF16), ((1,), (0,))),
                0.0,
            )
            return total, dot_total, out

        def back(part, grad_q):
            probs = s_ref[slot_of(part), lanes(part)] * scale[:, lanes(part)]
            grads = probs * (p_ref[slot_of(part), lanes(part)] - row_total[:, lanes(part)])
            grads = grads.astype(BF16)
            queries = pl.ds(base + part[2], TILE - part[2])
            grad_v = contract(probs.astype(BF16), g_ref[queries, :], ((1,), (0,)))
            grad_k = contract(grads, q_ref[queries, :], ((1,), (0,)))
            if part[3]:
                dv_ref[keys_of(part), :] = grad_v
                dk_ref[keys_of(part), :] = grad_k
            else:
                dv_ref[keys_of(part), :] += grad_v
                dk_ref[keys_of(part), :] += grad_k
            return grad_q + widen(
                part, contract(t_ref[64:128, keys_of(part)], grads, ((1,), (0,))), 0.0
            )

        def every(step, carry):
            for part in (*corner, *[(j * TILE, j * TILE, 0, False) for j in range(full)]):
                carry = step(part, carry)
            return carry

        top = every(score, jnp.full((1, TILE), -1e30, F32))
        zero = jnp.zeros((1, TILE), F32)
        total, dot_total, out = every(weigh, (zero, zero, jnp.zeros((64, TILE), F32)))
        scale = 1.0 / total
        row_total = dot_total * scale
        o_ref[0:64, pl.ds(base, TILE)] = (out * scale).astype(BF16)
        grad_q = every(back, jnp.zeros((64, TILE), F32)) * 0.125
        cosine = table_ref[0:8, pl.ds(last, TILE)]
        sine = table_ref[8:16, pl.ds(last, TILE)]
        o_ref[64:128, pl.ds(base, TILE)] = rotate_rows(grad_q, cosine, -sine).astype(BF16)

    for task in range(8):
        attend(task)

    def turn_back(task):
        base = task * TILE
        pos = base if task < 4 else 0
        cosine = table_ref[0:8, pl.ds(pos, TILE)]
        sine = table_ref[8:16, pl.ds(pos, TILE)]
        grad_k = dk_ref[pl.ds(base, TILE), :].T
        o_ref[128:192, pl.ds(base, TILE)] = rotate_rows(grad_k, cosine, -sine).astype(BF16)
        o_ref[192:256, pl.ds(base, TILE)] = dv_ref[pl.ds(base, TILE), :].T.astype(BF16)

    for task in range(8):
        turn_back(task)
    gw_ref[...] = jnp.zeros_like(gw_ref)
    go_ref[...] = jnp.zeros_like(go_ref)
    gb_ref[...] = jnp.zeros_like(gb_ref)
    gc_ref[...] = jnp.zeros_like(gc_ref)

    def collect(step, _):
        blocks = []
        for n in range(COLLECT):
            b = step * COLLECT + n
            post(b).start()
            blocks.append(o_ref[:, pl.ds(pl.multiple_of(logical(b) * TOK, TOK), TOK)])
        block = jnp.concatenate(blocks, 1)
        at = pl.multiple_of(step * COLLECT * TOK, TOK)
        grads = block[64:256]
        gw_ref[...] += contract(grads, rows_ref[pl.ds(at, COLLECT * TOK), :D], ((1,), (0,)))
        go_ref[...] += contract(block[0:64], rows_ref[pl.ds(at, COLLECT * TOK), D:], ((1,), (0,)))
        gb_ref[...] += contract(jnp.ones((8, COLLECT * TOK), BF16), grads, ((1,), (1,)))
        gc_ref[...] += jnp.broadcast_to(
            jnp.sum(grads.astype(F32), axis=1, keepdims=True), (192, 128)
        )
        return 0

    lax.fori_loop(0, SEQ_DEV // COLLECT, collect, 0)
    grad_ref[0:192, :] = gw_ref[...].astype(BF16)
    alive = which[1] == 1
    weights = w_ref[...].astype(F32)
    sums = gc_ref[:, 0:1]
    shift_grad = jnp.sum(sums * weights, axis=0, keepdims=True)
    gain_grad = jnp.sum(
        weights * (gw_ref[...] - sums * norm_ref[1:2, :]), axis=0, keepdims=True
    ) / norm_ref[0:1, :]
    bias_row = jnp.concatenate([gb_ref[0:1, :], jnp.zeros((1, D - 192), F32)], 1)
    own = jnp.concatenate([gain_grad, shift_grad, bias_row, jnp.zeros((5, D), F32)], 0)
    own = jnp.where(alive, own, 0.0)
    grad_ref[192:256, :] = go_ref[...].astype(BF16)
    grad_ref[256:272, :] = jnp.concatenate([own, extra_ref[...]], 0).astype(BF16)
    for b in range(SEQ_DEV):
        post(b).wait()


def one_head(ids, places, which, rows, table, output_weight, weight, bias, norm, extra):
    count = SEQ_DEV * TOK

    def whole(*shape):
        return pl.BlockSpec(shape, lambda s, *_: (0,) * len(shape))

    def cut(rows, n):
        return pl.BlockSpec((rows, 2 * DH), lambda s, l, p, w: (0, n * (H // 2) + w[0] // 2))

    return pl.pallas_call(
        head_kernel,
        out_shape=(
            jax.ShapeDtypeStruct((SEQ_DEV, 256, TOK), BF16),
            jax.ShapeDtypeStruct((272, D), BF16),
        ),
        grid_spec=pltpu.PrefetchScalarGridSpec(
            num_scalar_prefetch=3,
            grid=(1,),
            in_specs=[
                pl.BlockSpec(memory_space=pl.ANY),
                whole(16, 2048),
                pl.BlockSpec((DH, D), lambda s, l, p, w: (w[0], 0)),
                *[cut(D, n) for n in range(3)],
                *[cut(1, n) for n in range(3)],
                whole(8, D),
                whole(8, D),
            ],
            out_specs=(pl.BlockSpec(memory_space=pl.ANY), whole(272, D)),
            scratch_shapes=[
                pltpu.VMEM((count, 2 * D), BF16),
                pltpu.SemaphoreType.DMA((SEQ_DEV,)),
                pltpu.SemaphoreType.DMA((SEQ_DEV,)),
                pltpu.VMEM((192, D), BF16),
                pltpu.VMEM((192, 128), F32),
                pltpu.VMEM((256, count), BF16),
                pltpu.VMEM((count, DH), BF16),
                pltpu.VMEM((count, DH), BF16),
                pltpu.VMEM((count, DH), BF16),
                pltpu.VMEM((count, DH), BF16),
                pltpu.VMEM((4 * TILE, TILE), F32),
                pltpu.VMEM((4 * TILE, TILE), F32),
                pltpu.VMEM((count, DH), F32),
                pltpu.VMEM((count, DH), F32),
                pltpu.VMEM((256, count), BF16),
                pltpu.VMEM((192, D), F32),
                pltpu.VMEM((DH, D), F32),
                pltpu.VMEM((8, 192), F32),
                pltpu.VMEM((192, 128), F32),
            ],
        ),
        compiler_params=pltpu.CompilerParams(vmem_limit_bytes=56 * 2**20),
        cost_estimate=pl.CostEstimate(
            flops=24 * 10**9, bytes_accessed=12 * 10**6, transcendentals=4 * 10**6
        ),
    )(ids, places, which, rows, table, output_weight, *[weight] * 3, *[bias] * 3, norm, extra)


def rotary_table():
    freq = (1.0 / 10000.0 ** (np.arange(8, dtype=np.float64) * 2.0 / ROT)).astype(np.float32)
    angle = np.arange(2048, dtype=np.float32)[None, :] * freq[:, None]
    angle = angle.astype(np.float64)
    return np.concatenate([np.cos(angle), np.sin(angle)], 0).astype(np.float32)


def gelu_and_slope(values):
    cdf = 0.5 * (1.0 + lax.erf(values * np.float32(math.sqrt(0.5))))
    pdf = jnp.exp(-0.5 * values * values) * np.float32(1.0 / math.sqrt(2.0 * math.pi))
    return values * cdf, cdf + values * pdf


def feed_kernel(
    where, own_ref, other_ref, up_ref, down_ref, bias_ref, *refs,
):
    if len(refs) == 4:
        sum_ref, bias_sum_ref, rows_ref, total_ref = refs
    else:
        before_ref, sum_ref, bias_sum_ref, mine_ref, theirs_ref, total_ref = refs
    step = pl.program_id(0)
    second = jnp.concatenate([own_ref[:, :D], other_ref[:, :D]], 0)
    grads = jnp.concatenate([own_ref[:, D:], other_ref[:, D:]], 0)
    hidden = contract(second, up_ref[...], ((1,), (0,))) + bias_ref[...]
    active, slope = gelu_and_slope(hidden)
    active = active.astype(BF16)
    grad_hidden = (contract(grads, down_ref[...], ((1,), (1,))) * slope).astype(BF16)
    sum_ref[0] = contract(active, grads, ((0,), (0,))).astype(BF16)
    sum_ref[1] = contract(grad_hidden, second, ((0,), (0,))).astype(BF16)
    bias_sum_ref[...] = jnp.sum(grad_hidden.astype(F32), axis=0, keepdims=True)
    feed_part = contract(active, down_ref[...], ((1,), (0,)))
    back_part = contract(grad_hidden, up_ref[...], ((1,), (1,)))

    @pl.when(step == 0)
    def _():
        total_ref[:, :D] = feed_part
        total_ref[:, D:] = back_part

    @pl.when(step > 0)
    def _():
        total_ref[:, :D] += feed_part
        total_ref[:, D:] += back_part

    @pl.when(step == pl.num_programs(0) - 1)
    def _():
        if len(refs) == 4:
            rows_ref[...] = total_ref[...]
        else:
            mine_ref[...] = total_ref[:TOK, :] + before_ref[:TOK, :]
            theirs_ref[...] = (total_ref[TOK:, :] + before_ref[TOK:, :]).astype(BF16)


def feed_half(where, own, got, up_weight, down_weight, up_bias, *before):
    units, cut = FF // 4, FEED_CUT
    steps = units // cut
    rows = pl.BlockSpec((TOK, 2 * D), lambda s, w: (0, 0))
    both = pl.BlockSpec((2 * TOK, 2 * D), lambda s, w: (0, 0))
    if before:
        row_shapes = (
            jax.ShapeDtypeStruct((TOK, 2 * D), F32),
            jax.ShapeDtypeStruct((TOK, 2 * D), BF16),
        )
    else:
        row_shapes = (jax.ShapeDtypeStruct((2 * TOK, 2 * D), F32),)
    return pl.pallas_call(
        feed_kernel,
        out_shape=(
            jax.ShapeDtypeStruct((2, units, D), BF16),
            jax.ShapeDtypeStruct((1, units), F32),
            *row_shapes,
        ),
        grid_spec=pltpu.PrefetchScalarGridSpec(
            num_scalar_prefetch=1,
            grid=(steps,),
            in_specs=[
                rows,
                rows,
                pl.BlockSpec((D, cut), lambda s, w: (0, w[0] * steps + s)),
                pl.BlockSpec((cut, D), lambda s, w: (w[0] * steps + s, 0)),
                pl.BlockSpec((1, cut), lambda s, w: (0, w[0] * steps + s)),
                *[both] * len(before),
            ],
            out_specs=(
                pl.BlockSpec((2, cut, D), lambda s, w: (0, s, 0)),
                pl.BlockSpec((1, cut), lambda s, w: (0, s)),
                *([rows] * 2 if before else [both]),
            ),
            scratch_shapes=[pltpu.VMEM((2 * TOK, 2 * D), F32)],
        ),
        compiler_params=pltpu.CompilerParams(vmem_limit_bytes=58 * 2**20),
        cost_estimate=pl.CostEstimate(
            flops=4 * 10**9, bytes_accessed=8 * 10**6, transcendentals=10**6
        ),
    )(where, own, got, up_weight, down_weight, up_bias, *before)


def round_call(kernel, scalars, values, shapes, later=()):
    def whole(shape):
        return pl.BlockSpec(shape, lambda s, w: (0,) * len(shape))

    return pl.pallas_call(
        kernel,
        out_shape=tuple(jax.ShapeDtypeStruct(shape, BF16) for shape in shapes),
        grid_spec=pltpu.PrefetchScalarGridSpec(
            num_scalar_prefetch=1,
            grid=(1,),
            in_specs=[
                *[whole(value.shape) for value in values],
                *[pl.BlockSpec(memory_space=pl.ANY)] * len(later),
            ],
            out_specs=tuple(whole(shape) for shape in shapes),
        ),
        compiler_params=pltpu.CompilerParams(vmem_limit_bytes=58 * 2**20),
        cost_estimate=pl.CostEstimate(flops=0, bytes_accessed=0, transcendentals=0),
    )(scalars, *values, *later)


def hold_kernel(value_ref, *refs):
    del value_ref, refs


def hold(value, *later):
    return pl.pallas_call(
        hold_kernel,
        out_shape=jax.ShapeDtypeStruct(value.shape, value.dtype),
        in_specs=[pl.BlockSpec(memory_space=pl.ANY)] * (1 + len(later)),
        out_specs=pl.BlockSpec(memory_space=pl.ANY),
        input_output_aliases={0: 0},
        cost_estimate=pl.CostEstimate(flops=0, bytes_accessed=0, transcendentals=0),
    )(value, *later)


def quad_kernel(which, own_ref, *refs):
    values = [own_ref[...].astype(F32), *[ref[...].astype(F32) for ref in refs[:3]]]
    rows = []
    for k in range(4):
        row = values[3]
        for r in range(3):
            row = jnp.where((which[0] ^ k) == r, values[r], row)
        rows.append(row)
    refs[-1][...] = jnp.concatenate(rows, 1).astype(BF16)


def line_kernel(which, own_ref, *refs):
    rows = own_ref.shape[1]
    for r, ref in enumerate((own_ref, *refs[:3])):
        to = pl.multiple_of((which[0] ^ r) * rows, rows)
        refs[-1][:, pl.ds(to, rows), :] = ref[...]


def place_feed_kernel(where, mine_ref, theirs_ref, *refs):
    down_ref, up_ref = refs[-2:]

    def put(ref):
        down_ref[...] = ref[0].astype(F32)
        up_ref[...] = ref[1].astype(F32).T

    @pl.when(pl.program_id(0) == 0)
    def _():
        put(mine_ref)

    @pl.when(pl.program_id(0) == 1)
    def _():
        put(theirs_ref)


def place_feed(where, mine, theirs, placed):
    rows = FF // 8
    block = pl.BlockSpec((2, rows, D), lambda s, w: (0, 0, 0))
    kept = [pl.BlockSpec(memory_space=pl.ANY)] * len(placed)
    return pl.pallas_call(
        place_feed_kernel,
        out_shape=(
            jax.ShapeDtypeStruct((FF, D), F32),
            jax.ShapeDtypeStruct((D, FF), F32),
        ),
        grid_spec=pltpu.PrefetchScalarGridSpec(
            num_scalar_prefetch=1,
            grid=(2,),
            in_specs=[block, block, *kept],
            out_specs=(
                pl.BlockSpec((rows, D), lambda s, w: (w[s], 0)),
                pl.BlockSpec((D, rows), lambda s, w: (0, w[s])),
            ),
        ),
        input_output_aliases={3: 0, 4: 1} if placed else {},
        cost_estimate=pl.CostEstimate(flops=0, bytes_accessed=0, transcendentals=0),
    )(where, mine, theirs, *placed)


def place_heads_kernel(
    sums_ref, rest_ref, input_ref, output_ref,
    gain1_ref, shift1_ref, bias_ref, out_bias_ref, down_bias_ref, gain2_ref, shift2_ref, up_bias_ref,
):
    rows = sums_ref[...].reshape(H * DH, D).astype(F32)

    @pl.when(pl.program_id(1) < 3)
    def _():
        input_ref[...] = rows.T

    @pl.when(pl.program_id(1) == 3)
    def _():
        output_ref[...] = rows

    @pl.when((pl.program_id(0) == 0) & (pl.program_id(1) == 0))
    def _():
        rest = rest_ref[...].astype(F32)
        total = jnp.sum(rest, axis=0)
        for ref, n in (
            (gain1_ref, 0),
            (shift1_ref, 1),
            (out_bias_ref, 8),
            (down_bias_ref, 8),
            (gain2_ref, 9),
            (shift2_ref, 10),
        ):
            ref[...] = total[n : n + 1].reshape(D)
        bias = [rest[h, 2:3, n * DH : n * DH + DH] for n in range(3) for h in range(H)]
        bias_ref[...] = jnp.concatenate(bias, 1).reshape(3 * D)
        up = [sum(rest[d, n : n + 1] for d in range(c, SEQ_DEV, 2)) for c in (0, 1) for n in (11, 12)]
        up_bias_ref[...] = jnp.concatenate(up, 1).reshape(FF)


def place_heads(sums):
    sizes = (D, D, 3 * D, D, D, D, D, FF)
    return pl.pallas_call(
        place_heads_kernel,
        out_shape=(
            jax.ShapeDtypeStruct((D, 3 * D), F32),
            jax.ShapeDtypeStruct((D, D), F32),
            *[jax.ShapeDtypeStruct((size,), F32) for size in sizes],
        ),
        grid=(1, 4),
        in_specs=[
            pl.BlockSpec((H, DH, D), lambda p, n: (0, n, 0)),
            pl.BlockSpec((SEQ_DEV, 16, D), lambda p, n: (0, 16, 0)),
        ],
        out_specs=(
            pl.BlockSpec((D, D), lambda p, n: (0, jnp.minimum(n, 2))),
            pl.BlockSpec((H * DH, D), lambda p, n: (0, 0)),
            *[pl.BlockSpec((size,), lambda p, n: (0,)) for size in sizes],
        ),
        compiler_params=pltpu.CompilerParams(vmem_limit_bytes=58 * 2**20),
        cost_estimate=pl.CostEstimate(flops=0, bytes_accessed=0, transcendentals=0),
    )(sums, sums)


def norm_back(normal, rate, grad, gain):
    scaled = grad * gain
    return rate * (
        scaled
        - jnp.mean(scaled, axis=-1, keepdims=True)
        - normal * jnp.mean(scaled * normal, axis=-1, keepdims=True)
    )


def finish_kernel(
    back_ref, x_ref, grad_ref, normal_ref, rate_ref, parts_ref, gain1_ref, gain2_ref,
    out_bias_ref, down_bias_ref, out_weight_ref, in_weight_ref,
    result_ref, grad_x_ref,
):
    def row(ref):
        return ref[...].astype(F32).reshape(1, D)

    attended = jnp.concatenate([back_ref[h, :DH] for h in range(H)], 0)
    out = contract(attended, out_weight_ref[...], ((0,), (0,)))
    out = out + parts_ref[:, :D] + row(out_bias_ref) + row(down_bias_ref)
    result_ref[...] = (x_ref[...].astype(F32) + out).astype(BF16)
    mixed = jnp.concatenate(
        [back_ref[h, n * DH : (n + 1) * DH] for n in range(1, 4) for h in range(H)], 0
    )
    grad_first = contract(mixed, in_weight_ref[...], ((0,), (1,)))
    normal, rate = normal_ref[...], rate_ref[:, 0:1]
    grad_x_ref[...] = (
        grad_ref[...].astype(F32)
        + norm_back(normal, rate, grad_first, row(gain1_ref))
        + norm_back(normal, rate, parts_ref[:, D:], row(gain2_ref))
    )


def finish(back, *values):
    def whole(value):
        return pl.BlockSpec(value.shape, lambda s: (0,) * value.ndim)

    return pl.pallas_call(
        finish_kernel,
        out_shape=(
            jax.ShapeDtypeStruct((TOK, D), BF16),
            jax.ShapeDtypeStruct((TOK, D), F32),
        ),
        grid=(1,),
        in_specs=[
            pl.BlockSpec((H, 256, TOK), lambda s: (0, 0, 0)),
            *[whole(value) for value in values],
        ],
        out_specs=(
            pl.BlockSpec((TOK, D), lambda s: (0, 0)),
            pl.BlockSpec((TOK, D), lambda s: (0, 0)),
        ),
        compiler_params=pltpu.CompilerParams(vmem_limit_bytes=58 * 2**20),
        cost_estimate=pl.CostEstimate(flops=0, bytes_accessed=0, transcendentals=0),
    )(back, *values)


def body(
    tokens,
    sequence,
    positions,
    first_gain,
    first_shift,
    input_weight,
    input_bias,
    output_weight,
    output_bias,
    second_gain,
    second_shift,
    up_weight,
    up_bias,
    down_weight,
    down_bias,
    cotangent,
):
    at = here()
    seq = at["y"] * 4 + at["zl"] * 2 + at["c"]
    core = at["c"]
    grad_rows = cotangent[0]
    grad_float = grad_rows.astype(F32)

    with jax.named_scope("norms"):
        rows, own, normal, rate = norms(
            tokens[0], grad_rows, (first_gain, first_shift, second_gain, second_shift)
        )

    with jax.named_scope("gather_rows"):
        rows_all = lax.all_gather(rows, SEQ, axis=0, tiled=True)

    with jax.named_scope("feed"):
        first_bit, second_bit = ring_bits(at["x"], core)
        got = swap(own, other("c"))
        weights = (own, got, up_weight, down_weight, up_bias.astype(F32)[None])
        sent, sent_bias, before = feed_half((core * 2 + 1 - first_bit)[None], *weights)
        kept, kept_bias, parts, theirs = feed_half(
            (core * 2 + first_bit)[None], *weights, before
        )
        parts = parts + swap(theirs, other("c")).astype(F32)
        grad_second = parts[:, D:]
        extra = jnp.concatenate(
            [
                jnp.sum(grad_float, axis=0)[None],
                jnp.sum(grad_second * normal, axis=0)[None],
                jnp.sum(grad_second, axis=0)[None],
                jnp.where(first_bit == 0, kept_bias, sent_bias),
                jnp.where(first_bit == 0, sent_bias, kept_bias),
                jnp.zeros((3, D), F32),
            ],
            0,
        )

    with jax.named_scope("feed_scatter"):
        feed_sum = added(kept, swap(sent, ring_partner("x", 0)))
        got = swap(half(feed_sum, 1 - second_bit), ring_partner("x", 1))
        feed_sum = added(half(feed_sum, second_bit), got)
        feed_sum = feed_sum.reshape(2, 16, FF // 128, D).transpose(1, 0, 2, 3)
        spread = lax.all_to_all(feed_sum, ("y", "zl", "zh"), 0, 0, tiled=True)

    with jax.named_scope("head"):
        which = jnp.stack([jnp.minimum(seq, H - 1), (seq < H).astype(jnp.int32)])
        norm = jnp.stack([first_gain, first_shift] * 4).astype(F32)
        send, head_sum = one_head(
            sequence[0],
            positions[0],
            which.astype(jnp.int32),
            rows_all,
            jnp.asarray(rotary_table()),
            output_weight,
            input_weight,
            input_bias.astype(F32)[None],
            norm,
            after(extra, feed_sum),
        )

    def scalars(*values):
        return jnp.stack(values).astype(jnp.int32)

    with jax.named_scope("rounds"):
        def flipped(*axes):
            return lambda p: {**p, **{axis: 1 - p[axis] for axis in axes}}

        def along_y(r):
            return lambda p: {**p, "y": p["y"] ^ r}

        spread = hold(spread, head_sum)
        feed_sum = added(*[spread[n] for n in range(16)])
        (feed_sum,) = round_call(
            quad_kernel,
            scalars(at["zl"] * 2 + at["zh"]),
            (feed_sum, *[swap(feed_sum, flipped(*f)) for f in (("zh",), ("zl",), ("zl", "zh"))]),
            ((2, 96, D),),
        )
        head_sum = added(head_sum, swap(head_sum, other("zh")))
        got = [swap(feed_sum, along_y(r)) for r in (1, 2, 3)]
        (feed_sum,) = round_call(
            line_kernel, scalars(at["y"]), (feed_sum, *got), ((2, FF // 8, D),)
        )
        back = lax.all_to_all(hold(send, feed_sum), SEQ, 0, 0, tiled=True)
        for step in range(2):
            head_sum = added(head_sum, swap(head_sum, ring_partner("x", step)))
        one = swap(feed_sum, ring_partner("x", 1))
        two = swap(feed_sum, ring_partner("x", 0))
        sums = lax.all_gather(hold(head_sum, back, one, two), SEQ, axis=0)

    with jax.named_scope("heads_back"):
        result, grad_tokens = finish(
            back, tokens[0], grad_rows, normal, rate, parts, first_gain, second_gain,
            output_bias, down_bias, output_weight, input_weight,
        )
        result, grad_tokens = result[None], grad_tokens[None]

    with jax.named_scope("feed_gather"):
        blocks = [
            [c * 4 + ring_chunk(x, c) for x in ring_slots(at["x"], c)] for c in (core, 1 - core)
        ]
        where = [scalars(blocks[0][n], blocks[1][n]) for n in range(4)]
        last = swap(one, ring_partner("x", 0))
        theirs = swap(feed_sum, other("c"))
        placed = place_feed(where[0], hold(feed_sum, grad_tokens), theirs, ())
        placed = place_feed(where[1], one, swap(one, other("c")), placed)
        placed = place_feed(where[2], two, swap(two, other("c")), placed)
        last = hold(last, placed[0])
        placed = place_feed(where[3], last, swap(last, other("c")), placed)
        grad_down_weight, grad_up_weight = placed

    with jax.named_scope("head_place"):
        (
            grad_input_weight,
            grad_output_weight,
            grad_first_gain,
            grad_first_shift,
            grad_input_bias,
            grad_output_bias,
            grad_down_bias,
            grad_second_gain,
            grad_second_shift,
            grad_up_bias,
        ) = place_heads(sums)
    return (
        result,
        grad_tokens,
        grad_first_gain,
        grad_first_shift,
        grad_input_weight,
        grad_input_bias,
        grad_output_weight,
        grad_output_bias,
        grad_second_gain,
        grad_second_shift,
        grad_up_weight,
        grad_up_bias,
        grad_down_weight,
        grad_down_bias,
    )


def solution(mesh):
    mesh = jax.sharding.Mesh(mesh.devices.reshape(SIZES), AXES)
    split, groups = P(("x", "zh"), SEQ, None), P(("x", "zh"), None)
    in_specs = (split, groups, groups, *(P(),) * 12, split)
    out_specs = (split, split, *(P(),) * 12)
    return jax.shard_map(body, mesh=mesh, in_specs=in_specs, out_specs=out_specs, check_vma=False)
```

```python
import math

import jax
import jax.numpy as jnp
import numpy as np
from jax import lax
from jax.experimental import pallas as pl
from jax.experimental.pallas import tpu as pltpu
from jax.sharding import PartitionSpec as P

H = 12
DH = 64
D = 768
FF = 3072
ROT = 16
TOK = 256
SEQ_DEV = 16
LONG_BLOCKS = 8
EPS = 1e-05
F32 = jnp.float32
BF16 = jnp.bfloat16
TILE = 512
PROJECT = 4
COLLECT = 4
AHEAD = 8
FEED_CUT = 384
HEAD_ROWS = 272


AXES = ("y", "zl", "c", "x", "zh")
SIZES = (4, 2, 2, 4, 2)
SEQ = ("y", "zl", "c")


def place(index):
    at = {}
    for name, size in zip(reversed(AXES), reversed(SIZES)):
        index, at[name] = divmod(index, size)
    return at


def index_of(at):
    index = 0
    for name, size in zip(AXES, SIZES):
        index = index * size + at[name]
    return index


def swap(value, partner):
    pairs = [(i, index_of(partner(place(i)))) for i in range(math.prod(SIZES))]
    return lax.ppermute(value, AXES, pairs)


def here():
    return {name: lax.axis_index(name) for name in AXES}


def other(axis):
    return lambda at: {**at, axis: 1 - at[axis]}


def ring_next(i, core, step):
    near, far = i ^ 1, 3 - i
    if isinstance(core, int):
        return near if step == core else far
    return jnp.where(core == step, near, far)


def ring_partner(axis, step):
    return lambda at: {**at, axis: ring_next(at[axis], at["c"], step)}


def ring_bits(i, core):
    inner = ((i == 1) | (i == 2)).astype(jnp.int32)
    upper = (i >= 2).astype(jnp.int32)
    return jnp.where(core == 0, inner, upper), jnp.where(core == 0, upper, inner)


def ring_chunk(i, core):
    first, second = ring_bits(i, core)
    return first * 2 + second


def ring_slots(i, core):
    one, two = ring_next(i, core, 1), ring_next(i, core, 0)
    return [i, one, two, ring_next(two, core, 1)]


def added(*values):
    total = values[0].astype(F32)
    for value in values[1:]:
        total = total + value.astype(F32)
    return total.astype(BF16)


def half(value, which):
    rows = value.shape[1] // 2
    return lax.dynamic_slice_in_dim(value, which * rows, rows, 1)


def after(value, *earlier):
    return lax.optimization_barrier((value, *earlier))[0]


def norm_kernel(
    x_ref, grad_ref, gain1_ref, shift1_ref, gain2_ref, shift2_ref,
    rows_ref, own_ref, normal_ref, rate_ref,
):
    def row(ref):
        return ref[...].astype(F32).reshape(1, D)

    values = x_ref[...].astype(F32)
    centre = values - jnp.mean(values, axis=-1, keepdims=True)
    spread = jnp.mean(centre * centre, axis=-1, keepdims=True)
    rate = lax.rsqrt(spread + EPS)
    normal = centre * rate
    rows_ref[:, :D] = (normal * row(gain1_ref) + row(shift1_ref)).astype(BF16)
    own_ref[:, :D] = (normal * row(gain2_ref) + row(shift2_ref)).astype(BF16)
    rows_ref[:, D:] = grad_ref[...]
    own_ref[:, D:] = grad_ref[...]
    normal_ref[...] = normal
    rate_ref[...] = jnp.broadcast_to(rate, (TOK, 128))


def norms(x, grad_rows, gains):
    return pl.pallas_call(
        norm_kernel,
        out_shape=(
            jax.ShapeDtypeStruct((TOK, 2 * D), BF16),
            jax.ShapeDtypeStruct((TOK, 2 * D), BF16),
            jax.ShapeDtypeStruct((TOK, D), F32),
            jax.ShapeDtypeStruct((TOK, 128), F32),
        ),
        cost_estimate=pl.CostEstimate(
            flops=3 * 10**8, bytes_accessed=5 * 10**6, transcendentals=256
        ),
    )(x, grad_rows, *gains)


def contract(left, right, dims):
    return lax.dot_general(left, right, (dims, ((), ())), preferred_element_type=F32)


def rotate_rows(rows, cosine, sine):
    first, second = rows[0:8], rows[8:16]
    return jnp.concatenate(
        [first * cosine - second * sine, second * cosine + first * sine, rows[16:]], 0
    )


def head_kernel(
    ids, places, which,
    rows_hbm, table_ref, wo_ref, wq_ref, wk_ref, wv_ref, bq_ref, bk_ref, bv_ref, norm_ref, extra_ref,
    send_hbm, grad_ref,
    rows_ref, in_sem, out_sem, w_ref, bias_ref, t_ref, q_ref, k_ref, v_ref, g_ref, s_ref, p_ref, dk_ref, dv_ref, o_ref, gw_ref, go_ref, gb_ref, gc_ref,
):
    def place_block(b):
        return lax.div(places[b * TOK], TOK)

    def logical(b):
        ident = ids[b * TOK]
        return place_block(b) + jnp.where(ident == 0, 0, LONG_BLOCKS + 2 * (ident - 1))

    def fetch(b):
        at = pl.multiple_of(b * TOK, TOK)
        return pltpu.make_async_copy(
            rows_hbm.at[pl.ds(at, TOK)], rows_ref.at[pl.ds(at, TOK)], in_sem.at[b]
        )

    def post(b):
        frm = pl.multiple_of(logical(b) * TOK, TOK)
        return pltpu.make_async_copy(
            o_ref.at[:, pl.ds(frm, TOK)], send_hbm.at[b], out_sem.at[b]
        )

    for b in range(AHEAD):
        fetch(b).start()
    odd = which[0] % 2 == 1
    for n, (w, bias) in enumerate(((wq_ref, bq_ref), (wk_ref, bk_ref), (wv_ref, bv_ref))):
        block = jnp.where(odd, w[:, DH:].astype(F32), w[:, :DH].astype(F32))
        w_ref[n * DH : n * DH + DH, :] = block.T.astype(BF16)
        row = jnp.where(odd, bias[:, DH:], bias[:, :DH])
        bias_ref[n * DH : n * DH + DH, :] = jnp.broadcast_to(row, (128, DH)).T

    def project(step, _):
        for n in range(PROJECT):
            fetch(step * PROJECT + n).wait()

        for n in range(PROJECT):
            ahead = step * PROJECT + n + AHEAD

            @pl.when(ahead < SEQ_DEV)
            def _():
                fetch(ahead).start()

        at = pl.multiple_of(step * PROJECT * TOK, TOK)
        rows = rows_ref[pl.ds(at, PROJECT * TOK), :]
        mixed_all = contract(w_ref[...], rows[:, :D], ((1,), (1,))) + bias_ref[:, 0:1]
        grad_all = contract(wo_ref[...], rows[:, D:], ((1,), (1,)))
        for n in range(PROJECT):
            b = step * PROJECT + n
            to = pl.multiple_of(logical(b) * TOK, TOK)
            pos = pl.multiple_of(place_block(b) * TOK, TOK)
            cosine = table_ref[0:8, pl.ds(pos, TOK)]
            sine = table_ref[8:16, pl.ds(pos, TOK)]
            mixed = mixed_all[:, n * TOK : n * TOK + TOK]
            query = rotate_rows(mixed[0:64], cosine, sine) * 0.125
            key = rotate_rows(mixed[64:128], cosine, sine)
            parts = (query, key, mixed[128:192], grad_all[:, n * TOK : n * TOK + TOK])
            for m, (part, ref) in enumerate(zip(parts, (q_ref, k_ref, v_ref, g_ref))):
                part = part.astype(BF16)
                t_ref[m * 64 : m * 64 + 64, pl.ds(to, TOK)] = part
                ref[pl.ds(to, TOK), :] = part.T
        return 0

    lax.fori_loop(0, SEQ_DEV // PROJECT, project, 0)

    def attend(task):
        base = task * TILE
        full = task if task < 4 else 0
        last = full * TILE
        small = TILE // 2
        corner = (
            (base, last, 0, True),
            (base + small, last + small, small, True),
        )

        def keys_of(part):
            return pl.ds(part[0], small if part[3] else TILE)

        def slot_of(part):
            return pl.ds(part[1], small if part[3] else TILE)

        def lanes(part):
            return slice(part[2], TILE)

        def widen(part, value, fill):
            if part[2] == 0:
                return value
            return jnp.concatenate([jnp.full(value.shape, fill, F32), value], 1)

        q_t = t_ref[0:64, pl.ds(base, TILE)]
        g_t = t_ref[192:256, pl.ds(base, TILE)]

        def score(part, top):
            scores = contract(k_ref[keys_of(part), :], q_t[:, lanes(part)], ((1,), (0,)))
            if part[3]:
                key_at = lax.broadcasted_iota(jnp.int32, scores.shape, 0)
                query_at = lax.broadcasted_iota(jnp.int32, scores.shape, 1)
                scores = jnp.where(key_at <= query_at, scores, -1e30)
            s_ref[slot_of(part), lanes(part)] = scores
            return jnp.maximum(top, widen(part, jnp.max(scores, axis=0, keepdims=True), -1e30))

        def weigh(part, carry):
            total, dot_total, out = carry
            raised = jnp.exp(s_ref[slot_of(part), lanes(part)] - top[:, lanes(part)])
            s_ref[slot_of(part), lanes(part)] = raised
            grads = contract(v_ref[keys_of(part), :], g_t[:, lanes(part)], ((1,), (0,)))
            p_ref[slot_of(part), lanes(part)] = grads
            total = total + widen(part, jnp.sum(raised, axis=0, keepdims=True), 0.0)
            dot_total = dot_total + widen(
                part, jnp.sum(raised * grads, axis=0, keepdims=True), 0.0
            )
            out = out + widen(
                part,
                contract(t_ref[128:192, keys_of(part)], raised.astype(BF16), ((1,), (0,))),
                0.0,
            )
            return total, dot_total, out

        def back(part, grad_q):
            probs = s_ref[slot_of(part), lanes(part)] * scale[:, lanes(part)]
            grads = probs * (p_ref[slot_of(part), lanes(part)] - row_total[:, lanes(part)])
            grads = grads.astype(BF16)
            queries = pl.ds(base + part[2], TILE - part[2])
            grad_v = contract(probs.astype(BF16), g_ref[queries, :], ((1,), (0,)))
            grad_k = contract(grads, q_ref[queries, :], ((1,), (0,)))
            if part[3]:
                dv_ref[keys_of(part), :] = grad_v
                dk_ref[keys_of(part), :] = grad_k
            else:
                dv_ref[keys_of(part), :] += grad_v
                dk_ref[keys_of(part), :] += grad_k
            return grad_q + widen(
                part, contract(t_ref[64:128, keys_of(part)], grads, ((1,), (0,))), 0.0
            )

        def every(step, carry):
            for part in (*corner, *[(j * TILE, j * TILE, 0, False) for j in range(full)]):
                carry = step(part, carry)
            return carry

        top = every(score, jnp.full((1, TILE), -1e30, F32))
        zero = jnp.zeros((1, TILE), F32)
        total, dot_total, out = every(weigh, (zero, zero, jnp.zeros((64, TILE), F32)))
        scale = 1.0 / total
        row_total = dot_total * scale
        o_ref[0:64, pl.ds(base, TILE)] = (out * scale).astype(BF16)
        grad_q = every(back, jnp.zeros((64, TILE), F32)) * 0.125
        cosine = table_ref[0:8, pl.ds(last, TILE)]
        sine = table_ref[8:16, pl.ds(last, TILE)]
        o_ref[64:128, pl.ds(base, TILE)] = rotate_rows(grad_q, cosine, -sine).astype(BF16)

    for task in range(8):
        attend(task)

    def turn_back(task):
        base = task * TILE
        pos = base if task < 4 else 0
        cosine = table_ref[0:8, pl.ds(pos, TILE)]
        sine = table_ref[8:16, pl.ds(pos, TILE)]
        grad_k = dk_ref[pl.ds(base, TILE), :].T
        o_ref[128:192, pl.ds(base, TILE)] = rotate_rows(grad_k, cosine, -sine).astype(BF16)
        o_ref[192:256, pl.ds(base, TILE)] = dv_ref[pl.ds(base, TILE), :].T.astype(BF16)

    for task in range(8):
        turn_back(task)
    gw_ref[...] = jnp.zeros_like(gw_ref)
    go_ref[...] = jnp.zeros_like(go_ref)
    gb_ref[...] = jnp.zeros_like(gb_ref)
    gc_ref[...] = jnp.zeros_like(gc_ref)

    def collect(step, _):
        blocks = []
        for n in range(COLLECT):
            b = step * COLLECT + n
            post(b).start()
            blocks.append(o_ref[:, pl.ds(pl.multiple_of(logical(b) * TOK, TOK), TOK)])
        block = jnp.concatenate(blocks, 1)
        at = pl.multiple_of(step * COLLECT * TOK, TOK)
        grads = block[64:256]
        gw_ref[...] += contract(grads, rows_ref[pl.ds(at, COLLECT * TOK), :D], ((1,), (0,)))
        go_ref[...] += contract(block[0:64], rows_ref[pl.ds(at, COLLECT * TOK), D:], ((1,), (0,)))
        gb_ref[...] += contract(jnp.ones((8, COLLECT * TOK), BF16), grads, ((1,), (1,)))
        gc_ref[...] += jnp.broadcast_to(
            jnp.sum(grads.astype(F32), axis=1, keepdims=True), (192, 128)
        )
        return 0

    lax.fori_loop(0, SEQ_DEV // COLLECT, collect, 0)
    grad_ref[0:192, :] = gw_ref[...].astype(BF16)
    alive = which[1] == 1
    weights = w_ref[...].astype(F32)
    sums = gc_ref[:, 0:1]
    shift_grad = jnp.sum(sums * weights, axis=0, keepdims=True)
    gain_grad = jnp.sum(
        weights * (gw_ref[...] - sums * norm_ref[1:2, :]), axis=0, keepdims=True
    ) / norm_ref[0:1, :]
    bias_row = jnp.concatenate([gb_ref[0:1, :], jnp.zeros((1, D - 192), F32)], 1)
    own = jnp.concatenate([gain_grad, shift_grad, bias_row, jnp.zeros((5, D), F32)], 0)
    own = jnp.where(alive, own, 0.0)
    grad_ref[192:256, :] = go_ref[...].astype(BF16)
    grad_ref[256:272, :] = jnp.concatenate([own, extra_ref[...]], 0).astype(BF16)
    for b in range(SEQ_DEV):
        post(b).wait()


def one_head(ids, places, which, rows, table, output_weight, weight, bias, norm, extra):
    count = SEQ_DEV * TOK

    def whole(*shape):
        return pl.BlockSpec(shape, lambda s, *_: (0,) * len(shape))

    def cut(rows, n):
        return pl.BlockSpec((rows, 2 * DH), lambda s, l, p, w: (0, n * (H // 2) + w[0] // 2))

    return pl.pallas_call(
        head_kernel,
        out_shape=(
            jax.ShapeDtypeStruct((SEQ_DEV, 256, TOK), BF16),
            jax.ShapeDtypeStruct((272, D), BF16),
        ),
        grid_spec=pltpu.PrefetchScalarGridSpec(
            num_scalar_prefetch=3,
            grid=(1,),
            in_specs=[
                pl.BlockSpec(memory_space=pl.ANY),
                whole(16, 2048),
                pl.BlockSpec((DH, D), lambda s, l, p, w: (w[0], 0)),
                *[cut(D, n) for n in range(3)],
                *[cut(1, n) for n in range(3)],
                whole(8, D),
                whole(8, D),
            ],
            out_specs=(pl.BlockSpec(memory_space=pl.ANY), whole(272, D)),
            scratch_shapes=[
                pltpu.VMEM((count, 2 * D), BF16),
                pltpu.SemaphoreType.DMA((SEQ_DEV,)),
                pltpu.SemaphoreType.DMA((SEQ_DEV,)),
                pltpu.VMEM((192, D), BF16),
                pltpu.VMEM((192, 128), F32),
                pltpu.VMEM((256, count), BF16),
                pltpu.VMEM((count, DH), BF16),
                pltpu.VMEM((count, DH), BF16),
                pltpu.VMEM((count, DH), BF16),
                pltpu.VMEM((count, DH), BF16),
                pltpu.VMEM((4 * TILE, TILE), F32),
                pltpu.VMEM((4 * TILE, TILE), F32),
                pltpu.VMEM((count, DH), F32),
                pltpu.VMEM((count, DH), F32),
                pltpu.VMEM((256, count), BF16),
                pltpu.VMEM((192, D), F32),
                pltpu.VMEM((DH, D), F32),
                pltpu.VMEM((8, 192), F32),
                pltpu.VMEM((192, 128), F32),
            ],
        ),
        compiler_params=pltpu.CompilerParams(vmem_limit_bytes=56 * 2**20),
        cost_estimate=pl.CostEstimate(
            flops=24 * 10**9, bytes_accessed=12 * 10**6, transcendentals=4 * 10**6
        ),
    )(ids, places, which, rows, table, output_weight, *[weight] * 3, *[bias] * 3, norm, extra)


def rotary_table():
    freq = (1.0 / 10000.0 ** (np.arange(8, dtype=np.float64) * 2.0 / ROT)).astype(np.float32)
    angle = np.arange(2048, dtype=np.float32)[None, :] * freq[:, None]
    angle = angle.astype(np.float64)
    return np.concatenate([np.cos(angle), np.sin(angle)], 0).astype(np.float32)


def gelu_and_slope(values):
    cdf = 0.5 * (1.0 + lax.erf(values * np.float32(math.sqrt(0.5))))
    pdf = jnp.exp(-0.5 * values * values) * np.float32(1.0 / math.sqrt(2.0 * math.pi))
    return values * cdf, cdf + values * pdf


def feed_kernel(
    where, own_ref, other_ref, up_ref, down_ref, bias_ref, *refs,
):
    if len(refs) == 4:
        sum_ref, bias_sum_ref, rows_ref, total_ref = refs
    else:
        before_ref, sum_ref, bias_sum_ref, mine_ref, theirs_ref, total_ref = refs
    step = pl.program_id(0)
    second = jnp.concatenate([own_ref[:, :D], other_ref[:, :D]], 0)
    grads = jnp.concatenate([own_ref[:, D:], other_ref[:, D:]], 0)
    hidden = contract(second, up_ref[...], ((1,), (0,))) + bias_ref[...]
    active, slope = gelu_and_slope(hidden)
    active = active.astype(BF16)
    grad_hidden = (contract(grads, down_ref[...], ((1,), (1,))) * slope).astype(BF16)
    sum_ref[0] = contract(active, grads, ((0,), (0,))).astype(BF16)
    sum_ref[1] = contract(grad_hidden, second, ((0,), (0,))).astype(BF16)
    bias_sum_ref[...] = jnp.sum(grad_hidden.astype(F32), axis=0, keepdims=True)
    feed_part = contract(active, down_ref[...], ((1,), (0,)))
    back_part = contract(grad_hidden, up_ref[...], ((1,), (1,)))

    @pl.when(step == 0)
    def _():
        total_ref[:, :D] = feed_part
        total_ref[:, D:] = back_part

    @pl.when(step > 0)
    def _():
        total_ref[:, :D] += feed_part
        total_ref[:, D:] += back_part

    @pl.when(step == pl.num_programs(0) - 1)
    def _():
        if len(refs) == 4:
            rows_ref[...] = total_ref[...]
        else:
            mine_ref[...] = total_ref[:TOK, :] + before_ref[:TOK, :]
            theirs_ref[...] = (total_ref[TOK:, :] + before_ref[TOK:, :]).astype(BF16)


def feed_half(where, own, got, up_weight, down_weight, up_bias, *before):
    units, cut = FF // 4, FEED_CUT
    steps = units // cut
    rows = pl.BlockSpec((TOK, 2 * D), lambda s, w: (0, 0))
    both = pl.BlockSpec((2 * TOK, 2 * D), lambda s, w: (0, 0))
    if before:
        row_shapes = (
            jax.ShapeDtypeStruct((TOK, 2 * D), F32),
            jax.ShapeDtypeStruct((TOK, 2 * D), BF16),
        )
    else:
        row_shapes = (jax.ShapeDtypeStruct((2 * TOK, 2 * D), F32),)
    return pl.pallas_call(
        feed_kernel,
        out_shape=(
            jax.ShapeDtypeStruct((2, units, D), BF16),
            jax.ShapeDtypeStruct((1, units), F32),
            *row_shapes,
        ),
        grid_spec=pltpu.PrefetchScalarGridSpec(
            num_scalar_prefetch=1,
            grid=(steps,),
            in_specs=[
                rows,
                rows,
                pl.BlockSpec((D, cut), lambda s, w: (0, w[0] * steps + s)),
                pl.BlockSpec((cut, D), lambda s, w: (w[0] * steps + s, 0)),
                pl.BlockSpec((1, cut), lambda s, w: (0, w[0] * steps + s)),
                *[both] * len(before),
            ],
            out_specs=(
                pl.BlockSpec((2, cut, D), lambda s, w: (0, s, 0)),
                pl.BlockSpec((1, cut), lambda s, w: (0, s)),
                *([rows] * 2 if before else [both]),
            ),
            scratch_shapes=[pltpu.VMEM((2 * TOK, 2 * D), F32)],
        ),
        compiler_params=pltpu.CompilerParams(vmem_limit_bytes=58 * 2**20),
        cost_estimate=pl.CostEstimate(
            flops=4 * 10**9, bytes_accessed=8 * 10**6, transcendentals=10**6
        ),
    )(where, own, got, up_weight, down_weight, up_bias, *before)


def round_call(kernel, scalars, values, shapes, later=()):
    def whole(shape):
        return pl.BlockSpec(shape, lambda s, w: (0,) * len(shape))

    return pl.pallas_call(
        kernel,
        out_shape=tuple(jax.ShapeDtypeStruct(shape, BF16) for shape in shapes),
        grid_spec=pltpu.PrefetchScalarGridSpec(
            num_scalar_prefetch=1,
            grid=(1,),
            in_specs=[
                *[whole(value.shape) for value in values],
                *[pl.BlockSpec(memory_space=pl.ANY)] * len(later),
            ],
            out_specs=tuple(whole(shape) for shape in shapes),
        ),
        compiler_params=pltpu.CompilerParams(vmem_limit_bytes=58 * 2**20),
        cost_estimate=pl.CostEstimate(flops=0, bytes_accessed=0, transcendentals=0),
    )(scalars, *values, *later)


def hold_kernel(value_ref, *refs):
    del value_ref, refs


def hold(value, *later):
    return pl.pallas_call(
        hold_kernel,
        out_shape=jax.ShapeDtypeStruct(value.shape, value.dtype),
        in_specs=[pl.BlockSpec(memory_space=pl.ANY)] * (1 + len(later)),
        out_specs=pl.BlockSpec(memory_space=pl.ANY),
        input_output_aliases={0: 0},
        cost_estimate=pl.CostEstimate(flops=0, bytes_accessed=0, transcendentals=0),
    )(value, *later)


def total_of(*refs):
    total = refs[0][...].astype(F32)
    for ref in refs[1:]:
        total = total + ref[...].astype(F32)
    return total.astype(BF16)


def quad_kernel(which, own_ref, *refs):
    values = [own_ref[...].astype(F32), *[ref[...].astype(F32) for ref in refs[:3]]]
    rows = []
    for k in range(4):
        row = values[3]
        for r in range(3):
            row = jnp.where((which[0] ^ k) == r, values[r], row)
        rows.append(row)
    refs[-2][...] = jnp.concatenate(rows, 1).astype(BF16)
    refs[-1][...] = total_of(*refs[3:5])


def line_kernel(which, own_ref, *refs):
    rows = own_ref.shape[1]
    for r, ref in enumerate((own_ref, *refs[:3])):
        to = pl.multiple_of((which[0] ^ r) * rows, rows)
        refs[-2][:, pl.ds(to, rows), :] = ref[...]
    refs[-1][...] = total_of(*refs[3:7])


def place_feed_kernel(where, mine_ref, theirs_ref, *refs):
    down_ref, up_ref = refs[-2:]

    def put(ref):
        down_ref[...] = ref[0].astype(F32)
        up_ref[...] = ref[1].astype(F32).T

    @pl.when(pl.program_id(0) == 0)
    def _():
        put(mine_ref)

    @pl.when(pl.program_id(0) == 1)
    def _():
        put(theirs_ref)


def place_feed(where, mine, theirs, placed):
    rows = FF // 8
    block = pl.BlockSpec((2, rows, D), lambda s, w: (0, 0, 0))
    kept = [pl.BlockSpec(memory_space=pl.ANY)] * len(placed)
    return pl.pallas_call(
        place_feed_kernel,
        out_shape=(
            jax.ShapeDtypeStruct((FF, D), F32),
            jax.ShapeDtypeStruct((D, FF), F32),
        ),
        grid_spec=pltpu.PrefetchScalarGridSpec(
            num_scalar_prefetch=1,
            grid=(2,),
            in_specs=[block, block, *kept],
            out_specs=(
                pl.BlockSpec((rows, D), lambda s, w: (w[s], 0)),
                pl.BlockSpec((D, rows), lambda s, w: (0, w[s])),
            ),
        ),
        input_output_aliases={3: 0, 4: 1} if placed else {},
        cost_estimate=pl.CostEstimate(flops=0, bytes_accessed=7 * 10**6, transcendentals=0),
    )(where, mine, theirs, *placed)


def place_heads_kernel(
    sums_ref, rest_ref, input_ref, output_ref,
    gain1_ref, shift1_ref, bias_ref, out_bias_ref, down_bias_ref, gain2_ref, shift2_ref, up_bias_ref,
):
    rows = sums_ref[...].reshape(H * DH, D).astype(F32)

    @pl.when(pl.program_id(1) < 3)
    def _():
        input_ref[...] = rows.T

    @pl.when(pl.program_id(1) == 3)
    def _():
        output_ref[...] = rows

    @pl.when((pl.program_id(0) == 0) & (pl.program_id(1) == 0))
    def _():
        rest = rest_ref[...].astype(F32)
        total = jnp.sum(rest, axis=0)
        for ref, n in (
            (gain1_ref, 0),
            (shift1_ref, 1),
            (out_bias_ref, 8),
            (down_bias_ref, 8),
            (gain2_ref, 9),
            (shift2_ref, 10),
        ):
            ref[...] = total[n : n + 1].reshape(D)
        bias = [rest[h, 2:3, n * DH : n * DH + DH] for n in range(3) for h in range(H)]
        bias_ref[...] = jnp.concatenate(bias, 1).reshape(3 * D)
        up = [sum(rest[d, n : n + 1] for d in range(c, SEQ_DEV, 2)) for c in (0, 1) for n in (11, 12)]
        up_bias_ref[...] = jnp.concatenate(up, 1).reshape(FF)


def place_heads(sums):
    sizes = (D, D, 3 * D, D, D, D, D, FF)
    return pl.pallas_call(
        place_heads_kernel,
        out_shape=(
            jax.ShapeDtypeStruct((D, 3 * D), F32),
            jax.ShapeDtypeStruct((D, D), F32),
            *[jax.ShapeDtypeStruct((size,), F32) for size in sizes],
        ),
        grid=(1, 4),
        in_specs=[
            pl.BlockSpec((H, DH, D), lambda p, n: (0, n, 0)),
            pl.BlockSpec((SEQ_DEV, 16, D), lambda p, n: (0, 16, 0)),
        ],
        out_specs=(
            pl.BlockSpec((D, D), lambda p, n: (0, jnp.minimum(n, 2))),
            pl.BlockSpec((H * DH, D), lambda p, n: (0, 0)),
            *[pl.BlockSpec((size,), lambda p, n: (0,)) for size in sizes],
        ),
        compiler_params=pltpu.CompilerParams(vmem_limit_bytes=58 * 2**20),
        cost_estimate=pl.CostEstimate(flops=0, bytes_accessed=0, transcendentals=0),
    )(sums, sums)


def norm_back(normal, rate, grad, gain):
    scaled = grad * gain
    return rate * (
        scaled
        - jnp.mean(scaled, axis=-1, keepdims=True)
        - normal * jnp.mean(scaled * normal, axis=-1, keepdims=True)
    )


def finish_kernel(
    back_ref, x_ref, grad_ref, normal_ref, rate_ref, parts_ref, gain1_ref, gain2_ref,
    out_bias_ref, down_bias_ref, out_weight_ref, in_weight_ref,
    result_ref, grad_x_ref,
):
    def row(ref):
        return ref[...].astype(F32).reshape(1, D)

    attended = jnp.concatenate([back_ref[h, :DH] for h in range(H)], 0)
    out = contract(attended, out_weight_ref[...], ((0,), (0,)))
    out = out + parts_ref[:, :D] + row(out_bias_ref) + row(down_bias_ref)
    result_ref[...] = (x_ref[...].astype(F32) + out).astype(BF16)
    mixed = jnp.concatenate(
        [back_ref[h, n * DH : (n + 1) * DH] for n in range(1, 4) for h in range(H)], 0
    )
    grad_first = contract(mixed, in_weight_ref[...], ((0,), (1,)))
    normal, rate = normal_ref[...], rate_ref[:, 0:1]
    grad_x_ref[...] = (
        grad_ref[...].astype(F32)
        + norm_back(normal, rate, grad_first, row(gain1_ref))
        + norm_back(normal, rate, parts_ref[:, D:], row(gain2_ref))
    )


def finish(back, *values):
    def whole(value):
        return pl.BlockSpec(value.shape, lambda s: (0,) * value.ndim)

    return pl.pallas_call(
        finish_kernel,
        out_shape=(
            jax.ShapeDtypeStruct((TOK, D), BF16),
            jax.ShapeDtypeStruct((TOK, D), F32),
        ),
        grid=(1,),
        in_specs=[
            pl.BlockSpec((H, 256, TOK), lambda s: (0, 0, 0)),
            *[whole(value) for value in values],
        ],
        out_specs=(
            pl.BlockSpec((TOK, D), lambda s: (0, 0)),
            pl.BlockSpec((TOK, D), lambda s: (0, 0)),
        ),
        compiler_params=pltpu.CompilerParams(vmem_limit_bytes=58 * 2**20),
        cost_estimate=pl.CostEstimate(flops=0, bytes_accessed=0, transcendentals=0),
    )(back, *values)


def body(
    tokens,
    sequence,
    positions,
    first_gain,
    first_shift,
    input_weight,
    input_bias,
    output_weight,
    output_bias,
    second_gain,
    second_shift,
    up_weight,
    up_bias,
    down_weight,
    down_bias,
    cotangent,
):
    at = here()
    seq = at["y"] * 4 + at["zl"] * 2 + at["c"]
    core = at["c"]
    grad_rows = cotangent[0]
    grad_float = grad_rows.astype(F32)

    with jax.named_scope("norms"):
        rows, own, normal, rate = norms(
            tokens[0], grad_rows, (first_gain, first_shift, second_gain, second_shift)
        )

    with jax.named_scope("gather_rows"):
        rows_all = lax.all_gather(rows, SEQ, axis=0, tiled=True)

    with jax.named_scope("feed"):
        first_bit, second_bit = ring_bits(at["x"], core)
        got = swap(own, other("c"))
        weights = (own, got, up_weight, down_weight, up_bias.astype(F32)[None])
        sent, sent_bias, before = feed_half((core * 2 + 1 - first_bit)[None], *weights)
        kept, kept_bias, parts, theirs = feed_half(
            (core * 2 + first_bit)[None], *weights, before
        )
        parts = parts + swap(theirs, other("c")).astype(F32)
        grad_second = parts[:, D:]
        extra = jnp.concatenate(
            [
                jnp.sum(grad_float, axis=0)[None],
                jnp.sum(grad_second * normal, axis=0)[None],
                jnp.sum(grad_second, axis=0)[None],
                jnp.where(first_bit == 0, kept_bias, sent_bias),
                jnp.where(first_bit == 0, sent_bias, kept_bias),
                jnp.zeros((3, D), F32),
            ],
            0,
        )

    with jax.named_scope("feed_scatter"):
        feed_sum = added(kept, swap(sent, ring_partner("x", 0)))
        got = swap(half(feed_sum, 1 - second_bit), ring_partner("x", 1))
        feed_sum = added(half(feed_sum, second_bit), got)
        feed_sum = feed_sum.reshape(2, 16, FF // 128, D).transpose(1, 0, 2, 3)
        spread = lax.all_to_all(feed_sum, ("y", "zl", "zh"), 0, 0, tiled=True)

    with jax.named_scope("head"):
        which = jnp.stack([jnp.minimum(seq, H - 1), (seq < H).astype(jnp.int32)])
        norm = jnp.stack([first_gain, first_shift] * 4).astype(F32)
        send, head_sum = one_head(
            sequence[0],
            positions[0],
            which.astype(jnp.int32),
            rows_all,
            jnp.asarray(rotary_table()),
            output_weight,
            input_weight,
            input_bias.astype(F32)[None],
            norm,
            after(extra, feed_sum),
        )

    def scalars(*values):
        return jnp.stack(values).astype(jnp.int32)

    with jax.named_scope("rounds"):
        def flipped(*axes):
            return lambda p: {**p, **{axis: 1 - p[axis] for axis in axes}}

        def along(axis, r):
            return lambda p: {**p, axis: p[axis] ^ r}

        head_sum = hold(head_sum, spread)
        feed_sum = added(*[spread[n] for n in range(16)])
        feed_sum, head_sum = round_call(
            quad_kernel,
            scalars(at["zl"] * 2 + at["zh"]),
            (
                feed_sum,
                *[swap(feed_sum, flipped(*f)) for f in (("zh",), ("zl",), ("zl", "zh"))],
                head_sum,
                swap(head_sum, flipped("zh")),
            ),
            ((2, 96, D), (HEAD_ROWS, D)),
        )
        feed_sum, head_sum = round_call(
            line_kernel,
            scalars(at["y"]),
            (
                feed_sum,
                *[swap(feed_sum, along("y", r)) for r in (1, 2, 3)],
                head_sum,
                *[swap(head_sum, along("x", r)) for r in (1, 2, 3)],
            ),
            ((2, FF // 8, D), (HEAD_ROWS, D)),
        )
        back = lax.all_to_all(hold(send, feed_sum), SEQ, 0, 0, tiled=True)
        one = swap(feed_sum, ring_partner("x", 1))
        two = swap(feed_sum, ring_partner("x", 0))
        sums = lax.all_gather(head_sum, SEQ, axis=0)

    with jax.named_scope("feed_gather"):
        blocks = [
            [c * 4 + ring_chunk(x, c) for x in ring_slots(at["x"], c)] for c in (core, 1 - core)
        ]
        where = [scalars(blocks[0][n], blocks[1][n]) for n in range(4)]
        theirs = swap(feed_sum, other("c"))
        placed = place_feed(where[0], feed_sum, theirs, ())
        one = hold(one, placed[0])
        last = swap(one, ring_partner("x", 0))
        placed = place_feed(where[1], one, swap(one, other("c")), placed)
        placed = place_feed(where[2], two, swap(two, other("c")), placed)
        with jax.named_scope("heads_back"):
            result, grad_tokens = finish(
                hold(back, placed[0], last), tokens[0], grad_rows, normal, rate, parts, first_gain, second_gain,
                output_bias, down_bias, output_weight, input_weight,
            )
            result, grad_tokens = result[None], grad_tokens[None]
        last = hold(last, grad_tokens)
        placed = place_feed(where[3], last, swap(last, other("c")), placed)
        grad_down_weight, grad_up_weight = placed

    with jax.named_scope("head_place"):
        (
            grad_input_weight,
            grad_output_weight,
            grad_first_gain,
            grad_first_shift,
            grad_input_bias,
            grad_output_bias,
            grad_down_bias,
            grad_second_gain,
            grad_second_shift,
            grad_up_bias,
        ) = place_heads(sums)
    return (
        result,
        grad_tokens,
        grad_first_gain,
        grad_first_shift,
        grad_input_weight,
        grad_input_bias,
        grad_output_weight,
        grad_output_bias,
        grad_second_gain,
        grad_second_shift,
        grad_up_weight,
        grad_up_bias,
        grad_down_weight,
        grad_down_bias,
    )


def solution(mesh):
    mesh = jax.sharding.Mesh(mesh.devices.reshape(SIZES), AXES)
    split, groups = P(("x", "zh"), SEQ, None), P(("x", "zh"), None)
    in_specs = (split, groups, groups, *(P(),) * 12, split)
    out_specs = (split, split, *(P(),) * 12)
    return jax.shard_map(body, mesh=mesh, in_specs=in_specs, out_specs=out_specs, check_vma=False)
```
